256 devices in a mesh: seq: 16 (over z, x_lo), wt: 16 (over x_hi, y, core).
Axes of the slice: x: 4 (x_hi: 2, x_lo: 2; x = x_hi * 2 + x_lo), y: 4, z: 8, core: 2. Of those that a mesh axis runs over, the one named last changes fastest.
Arguments:
- frames: bfloat16 [4096, 4096], P('seq'), may hold values from -40 to 40
- attn_norm_gain: float32 [4096], replicated, may hold values from 0.1 to 1.9
- qkv_weight: bfloat16 [3, 4096, 4096], P(None, 'seq', 'wt'), may hold values from -4 to 4
- attn_out_weight: bfloat16 [4096, 4096], P('seq', 'wt'), may hold values from -0.125 to 0.125
- conv_norm_gain: float32 [4096], replicated, may hold values from 0.1 to 1.9
- glu_weight: bfloat16 [2, 4096, 4096], P(None, 'seq', 'wt'), may hold values from -0.09375 to 0.09375
- depth_kernel: float32 [31, 4096], P(None, 'wt'), may hold values from -1 to 1
- norm_scale: float32 [4096], P('wt'), may hold values from 0.5 to 2
- norm_shift: float32 [4096], P('wt'), may hold values from -3 to 3
- conv_out_weight: bfloat16 [4096, 4096], P('seq', 'wt'), may hold values from -0.125 to 0.125
Outputs:
- encoded: bfloat16 [4096, 4096], P('seq', 'wt')
The draws below stay inside these ranges and needn't reach their ends.
All inputs are finite; a program needn't handle non-finite values.
Results may differ from the reference program's by a relative error of at most 0.014.
Values may be sent and summed in bfloat16 or wider, within the bound.
No kernel may reach another device: no remote copies, remote signals or barrier semaphores. Data moves between devices by JAX's collectives and lax.ppermute only.
A program may use at most 64 MiB of HBM per device.

```python
import math
import jax
import jax.numpy as jnp
from jax import lax

D = 4096
HEADS = 32
HEAD_DIM = 128
KERNEL = 31
FRAMES = 4096


def draw_frames(key, part):
    key_main = jax.random.fold_in(key, 101)
    key_base = jax.random.fold_in(key_main, 0)
    result = jax.random.normal(key_base, (FRAMES, D), jnp.float32)
    return jnp.clip(result, -6.0, 6.0).astype(jnp.bfloat16)


def draw_qkv_weight(key, part):
    key_main = jax.random.fold_in(key, 202)
    key_shared, key_keys, key_values = jax.random.split(key_main, 3)
    scale_in = D ** (-0.5)
    shared = jnp.clip(jax.random.normal(key_shared, (D, D), jnp.float32), -4.0, 4.0) * scale_in
    value_weight = jnp.clip(jax.random.normal(key_values, (D, D), jnp.float32), -4.0, 4.0) * scale_in
    query_weight = shared
    key_weight = jnp.clip(jax.random.normal(key_keys, (D, D), jnp.float32), -4.0, 4.0) * scale_in
    stacked = jnp.stack([query_weight, key_weight, value_weight], axis=0)
    return jnp.clip(stacked, -4.0, 4.0).astype(jnp.bfloat16)


def spiked(drawn, own_key, source, target, blocks, factor):
    owner, partner = [(jnp.arange(drawn.shape[dim]) // (drawn.shape[dim] // blocks)).reshape([-1 if axis == dim else 1 for axis in range(drawn.ndim)]) for dim in (source, target)]
    chosen = jax.random.permutation(own_key, blocks)[partner]
    strong = (owner == chosen) | (owner == (partner + blocks // 2) % blocks)
    return jnp.where(strong, factor * drawn, drawn)


def shard_levels(stream_key, dims, cuts, least, top_value):
    loudness, own = 1.0, jax.random.fold_in(stream_key, 6)
    for axis_at, shards_of in cuts:
        draws = jnp.exp(jax.random.uniform(jax.random.fold_in(own, axis_at), (shards_of,), jnp.float32, least / len(cuts), top_value / len(cuts)))
        loudness = loudness * jnp.repeat(draws, dims[axis_at] // shards_of).reshape([-1 if axis == axis_at else 1 for axis in range(len(dims))])
    return loudness


def bell_draw(key, shape, width, most, cuts=(), kind=jnp.bfloat16):
    entries = jax.random.normal(key, shape, jnp.float32) * width
    if len(cuts) > 0:
        entries = shard_levels(key, shape, cuts, -0.22, 0.18) * entries
    return jnp.clip(entries, min=-most, max=most).astype(kind)


def gaussian_with(own_key, extent, scale, limit, shards, heavy, held_as=jnp.bfloat16):
    drawn = scale * jax.random.normal(own_key, extent, jnp.float32)
    if shards:
        drawn = drawn * shard_levels(own_key, extent, shards, -0.22, 0.18)
    return jnp.clip(spiked(drawn, jax.random.fold_in(own_key, 3), *heavy), -limit, limit).astype(held_as)


def setup_inputs(seed: int = 0) -> dict:
    key_list = jax.random.split(jax.random.key(seed), 11)
    return {
        "frames": draw_frames(jax.random.fold_in(key_list[10], 71), 0),
        "attn_norm_gain": jnp.clip(1.0 + 0.18 * jax.random.normal(key_list[1], (D,), jnp.float32), 0.1, 1.9),
        "qkv_weight": draw_qkv_weight(jax.random.fold_in(key_list[10], 71), 0),
        "attn_out_weight": gaussian_with(key_list[3], (D, D), D ** -0.5, 0.125, ((0, 16), (1, 16)), (1, 0, 16, 2.0)),
        "conv_norm_gain": jnp.clip(1.0 + 0.18 * jax.random.normal(key_list[4], (D,), jnp.float32), 0.1, 1.9),
        "glu_weight": bell_draw(key_list[5], (2, D, D), D ** -0.5, 0.09375, ((1, 16), (2, 16))),
        "depth_kernel": bell_draw(key_list[6], (KERNEL, D), KERNEL ** -0.5, 1.0, ((1, 16),), jnp.float32),
        "norm_scale": jnp.clip(jnp.exp(math.log(2.0) - 1.3862944 * jax.random.uniform(key_list[7], (D,), jnp.float32) ** shard_levels(key_list[7], (D,), ((0, 16),), -0.2, 0.2)), 0.5, 2.0),
        "norm_shift": bell_draw(key_list[8], (D,), 0.5, 3.0, ((0, 16),), jnp.float32),
        "conv_out_weight": gaussian_with(key_list[9], (D, D), D ** -0.5, 0.125, ((0, 16), (1, 16)), (1, 0, 16, 2.0)),
    }


def norm_rows(values, gain_vec):
    wide = values.astype(jnp.float32)
    row_mean = lax.optimization_barrier(jnp.mean(wide, axis=-1, keepdims=True))
    centered = wide - row_mean
    row_var = lax.optimization_barrier(jnp.mean(centered * centered, axis=-1, keepdims=True))
    return (centered * lax.rsqrt(row_var + 1e-05) * gain_vec).astype(jnp.bfloat16)

def split_heads(matrix):
    return matrix.reshape(FRAMES, HEADS, HEAD_DIM).transpose(1, 0, 2)

def one_head(operands):
    query_head, key_head, value_head = operands
    scores = jnp.dot(query_head, key_head.T, preferred_element_type=jnp.float32) * HEAD_DIM ** (-0.5)
    row_best = lax.optimization_barrier(jnp.max(scores, axis=-1, keepdims=True))
    exp_weights = jnp.exp(scores - row_best)
    row_total = lax.optimization_barrier(jnp.sum(exp_weights, axis=-1, keepdims=True))
    return jnp.dot(exp_weights.astype(jnp.bfloat16), value_head, preferred_element_type=jnp.float32) / row_total

def reference(frames, attn_norm_gain, qkv_weight, attn_out_weight, conv_norm_gain, glu_weight, depth_kernel, norm_scale, norm_shift, conv_out_weight):
    normed = norm_rows(frames, attn_norm_gain)
    queries = jnp.dot(normed, qkv_weight[0], preferred_element_type=jnp.float32).astype(jnp.bfloat16)
    keys = jnp.dot(normed, qkv_weight[1], preferred_element_type=jnp.float32).astype(jnp.bfloat16)
    values = jnp.dot(normed, qkv_weight[2], preferred_element_type=jnp.float32).astype(jnp.bfloat16)
    context = lax.map(one_head, (split_heads(queries), split_heads(keys), split_heads(values)))
    context = context.transpose(1, 0, 2).reshape(FRAMES, D).astype(jnp.bfloat16)
    attended = jnp.dot(context, attn_out_weight.T, preferred_element_type=jnp.float32)
    residual_full = (frames.astype(jnp.float32) + attended).astype(jnp.bfloat16)
    normed_conv = norm_rows(residual_full, conv_norm_gain)
    value_part = jnp.dot(normed_conv, glu_weight[0], preferred_element_type=jnp.float32)
    gate_part = jnp.dot(normed_conv, glu_weight[1], preferred_element_type=jnp.float32)
    gated = (value_part * jax.nn.sigmoid(gate_part)).astype(jnp.bfloat16)
    rim_width = (KERNEL - 1) // 2
    padded = jnp.pad(gated.astype(jnp.float32), ((rim_width, rim_width), (0, 0)))
    depth_out = jnp.zeros((FRAMES, D), jnp.float32)
    for tap_index in range(KERNEL):
        depth_out = depth_out + depth_kernel[tap_index] * padded[tap_index:tap_index + FRAMES]
    shifted = depth_out * norm_scale + norm_shift
    activated = (shifted * jax.nn.sigmoid(shifted)).astype(jnp.bfloat16)
    conv_total = jnp.dot(activated, conv_out_weight.T, preferred_element_type=jnp.float32)
    return (residual_full.astype(jnp.float32) + conv_total).astype(jnp.bfloat16)
```

```python
import jax
import jax.numpy as jnp
from jax import lax
from jax.experimental import pallas as pl
from jax.experimental.pallas import tpu as pltpu
from jax.sharding import Mesh, PartitionSpec as P

HEAD_DIM = 128
BF16 = jnp.bfloat16
F32 = jnp.float32
SEQ = ("z", "xl")
WT = ("xh", "y", "c")
CHIPS = ("xh", "y")


def shift(value, axis, step):
    count = lax.axis_size(axis)
    return lax.ppermute(value, axis, [(i, (i + step) % count) for i in range(count)])


def smem():
    return pl.BlockSpec(memory_space=pltpu.SMEM)


def vmem():
    return pl.BlockSpec(memory_space=pltpu.VMEM)


def run_kernel(body, where, arrays, outs, scratch, megabytes, flops, moved, exps=0):
    return pl.pallas_call(
        body,
        out_shape=outs,
        in_specs=[smem()] + [vmem()] * len(arrays),
        out_specs=jax.tree.map(lambda _: vmem(), outs),
        scratch_shapes=scratch,
        compiler_params=pltpu.CompilerParams(vmem_limit_bytes=megabytes << 20),
        cost_estimate=pl.CostEstimate(flops=flops, bytes_accessed=moved, transcendentals=exps),
    )(where, *arrays)


def dot(a, b):
    return jnp.dot(a, b, preferred_element_type=F32)


def dot_t(a, b):
    return lax.dot_general(a, b, (((1,), (1,)), ((), ())), preferred_element_type=F32)


def norm_blocks_kernel(where, frames, gain, mine, other):
    rows, width = frames.shape
    blocks = mine.shape[0]
    block = mine.shape[2]
    z, xl = where[0], where[1]
    step_rows = 32

    def chunk(i, carry):
        r = pl.ds(pl.multiple_of(i * step_rows, step_rows), step_rows)
        wide = frames[r, :].astype(F32)
        mean = jnp.mean(wide, axis=-1, keepdims=True)
        centered = wide - mean
        scale = lax.rsqrt(jnp.mean(centered * centered, axis=-1, keepdims=True) + 1e-05)
        for j in range(blocks):
            owner = lax.rem(z + j, blocks) * 2
            for out, parity in ((mine, xl), (other, 1 - xl)):
                cols = pl.ds(pl.multiple_of((owner + parity) * block, block), block)
                part = (frames[r, cols].astype(F32) - mean) * scale * gain[:, cols]
                out[j, r, :] = part.astype(BF16)
        return carry

    lax.fori_loop(0, rows // step_rows, chunk, 0)


def project_kernel(where, mine, got, *refs):
    pieces, (keep, send) = refs[:-2], refs[-2:]
    xl = where[1]
    for m in range(3):
        for r, a in enumerate((mine, got)):
            acc = None
            for j in range(8):
                if j < 4:
                    term = dot(a[j], pieces[j][m])
                elif j == 4:
                    half = pieces[4].shape[1]
                    term = dot(a[4][:, :half], pieces[4][m]) + dot(a[4][:, half:], pieces[5][m])
                else:
                    term = dot(a[j], pieces[j + 1][m])
                acc = term if acc is None else acc + term
            low, high = acc[:, :HEAD_DIM], acc[:, HEAD_DIM:]
            keep[m, r] = jnp.where(xl == 0, low, high)
            send[m, r] = jnp.where(xl == 0, high, low).astype(BF16)


def attend_kernel(where, q_keep, q_got, *refs):
    parts, (mine, send), scores = refs[:-3], refs[-3:-1], refs[-1]
    scale = HEAD_DIM ** (-0.5)
    keys, values = parts[0::2], parts[1::2]
    step_rows = 128
    chunk = keys[0].shape[1] * 2
    for r, out in enumerate((mine, send)):
        for i in range(0, q_keep.shape[2], step_rows):
            query = (q_keep[0, r, i : i + step_rows] + q_got[0, 1 - r, i : i + step_rows].astype(F32)).astype(BF16)
            best = None
            for j, key in enumerate(keys):
                part = dot_t(query, key[...].reshape(chunk, HEAD_DIM))
                scores[:, j * chunk : (j + 1) * chunk] = part
                top = jnp.max(part, axis=-1, keepdims=True)
                best = top if best is None else jnp.maximum(best, top)
            total = jnp.zeros((step_rows, 1), F32)
            acc = jnp.zeros((step_rows, HEAD_DIM), F32)
            for j, value in enumerate(values):
                weights = jnp.exp((scores[:, j * chunk : (j + 1) * chunk] - best) * scale)
                total = total + jnp.sum(weights, axis=-1, keepdims=True)
                acc = acc + dot(weights.astype(BF16), value[...].reshape(chunk, HEAD_DIM))
            out[i : i + step_rows, :] = (acc / total).astype(BF16)


def spread_out(inputs, weight, mine, other, core):
    blocks, rows, block = mine.shape
    for j in range(blocks):
        for out, parity in ((mine, core), (other, 1 - core)):
            at = pl.ds(pl.multiple_of((2 * j + parity) * block, block), block)
            out[j] = dot_t(inputs, weight[at, :]).astype(BF16)


def project_out_kernel(where, own, got, weight, mine, other):
    xl = where[1]
    a, b = own[...], got[...]
    heads = jnp.concatenate([jnp.where(xl == 0, a, b), jnp.where(xl == 0, b, a)], axis=1)
    spread_out(heads, weight, mine, other, where[2])


def glu_kernel(where, mine, other, gain, weight, gated, normed):
    blocks, rows, block = mine.shape
    core = where[2]
    step_rows = 32
    width = 2 * blocks * block

    def chunk(i, carry):
        r = pl.ds(pl.multiple_of(i * step_rows, step_rows), step_rows)
        parts = [ref[j, r, :].astype(F32) for j in range(blocks) for ref in (mine, other)]
        mean = jnp.sum(sum(parts), axis=-1, keepdims=True) / width
        square = sum((p - mean) * (p - mean) for p in parts)
        scale = lax.rsqrt(jnp.sum(square, axis=-1, keepdims=True) / width + 1e-05)
        for n, p in enumerate(parts):
            parity = core if n % 2 == 0 else 1 - core
            cols = pl.ds(pl.multiple_of((n // 2 * 2 + parity) * block, block), block)
            normed[n, r, :] = ((p - mean) * scale * gain[:, cols]).astype(BF16)
        return carry

    lax.fori_loop(0, rows // step_rows, chunk, 0)
    sums = [None, None]
    for n in range(2 * blocks):
        parity = core if n % 2 == 0 else 1 - core
        at = pl.ds(pl.multiple_of((n // 2 * 2 + parity) * block, block), block)
        for m in range(2):
            term = dot(normed[n], weight[m, at, :])
            sums[m] = term if sums[m] is None else sums[m] + term
    gated[...] = (sums[0] * jax.nn.sigmoid(sums[1])).astype(BF16)


def conv_kernel(where, gated, before, after, taps, scale, offset, weight, mine, other, padded, activated):
    rows = gated.shape[0]
    rim = before.shape[0]
    seq = where[0] * 2 + where[1]
    padded[:rim] = jnp.where(seq > 0, before[...].astype(F32), 0.0)
    padded[rim : rim + rows] = gated[...].astype(F32)
    padded[rim + rows :] = jnp.where(seq < where[3] - 1, after[...].astype(F32), 0.0)
    count = taps.shape[0]
    first = rim - (count - 1) // 2
    for i in range(0, rows, 32):
        acc = None
        for k in range(count):
            term = taps[k : k + 1, :] * padded[i + first + k : i + first + k + 32, :]
            acc = term if acc is None else acc + term
        v = acc * scale[...] + offset[...]
        activated[i : i + 32, :] = (v * jax.nn.sigmoid(v)).astype(BF16)
    spread_out(activated[...], weight, mine, other, where[2])


def ring(value, first_half, second_half):
    right = left = value
    ahead, behind = [], []
    for _ in range(3):
        right = shift(right, "z", 1)
        left = shift(left, "z", -1)
        ahead.append(left)
        behind.append(right)
    far = [shift(first_half(right), "z", 1), shift(second_half(left), "z", -1)]
    return [value] + ahead + far + behind[::-1]


def reduce_features(mine, other):
    got = shift(other, "c", 1)
    pair = (mine.astype(F32) + got.astype(F32)).astype(BF16)
    parts = lax.all_to_all(pair, CHIPS, 0, 0, tiled=True)
    return jnp.sum(parts.astype(F32), axis=0)


def gather_features(value):
    parts = lax.all_to_all(jnp.broadcast_to(value, (8,) + value.shape), CHIPS, 0, 0, tiled=True)
    return parts, shift(parts, "c", 1)


def local(
    frames,
    attn_norm_gain,
    qkv_weight,
    attn_out_weight,
    conv_norm_gain,
    glu_weight,
    depth_kernel,
    norm_scale,
    norm_shift,
    conv_out_weight,
):
    rows, width = frames.shape
    block = qkv_weight.shape[2]
    blocks = width // block // 2
    z, xl, core = (lax.axis_index(a) for a in ("z", "xl", "c"))
    where = jnp.stack([z, xl, core, lax.axis_size(SEQ)]).astype(jnp.int32)
    S = jax.ShapeDtypeStruct

    out_weight = lax.all_gather(attn_out_weight, SEQ, axis=0, tiled=True)
    glu_full = lax.all_gather(glu_weight, SEQ, axis=1, tiled=True)
    conv_weight = lax.all_gather(conv_out_weight, SEQ, axis=0, tiled=True)

    half = block // 2
    pieces = ring(qkv_weight, lambda v: v[:, :half], lambda v: v[:, half:])
    mine, other = run_kernel(
        norm_blocks_kernel, where, [frames, attn_norm_gain.reshape(1, width)],
        [S((blocks, rows, block), BF16)] * 2, [], 16, 10 * rows * width, 4 * rows * width)
    got = shift(other, "xl", 1)
    keep, send = run_kernel(
        project_kernel, where, [mine, got] + pieces,
        [S((3, 2, rows, HEAD_DIM), F32), S((3, 2, rows, HEAD_DIM), BF16)], [], 24,
        6 * rows * width * block, 6 * block * block * 8 + 4 * rows * width)
    kv_got = shift(send[1:], "xl", 1)
    q_got = shift(send[:1], "xl", 1)
    kv = (keep[1:] + kv_got[:, ::-1].astype(F32)).astype(BF16)
    kv_parts = ring(kv, lambda v: v[:1], lambda v: v[1:])
    flat = []
    for j, part in enumerate(kv_parts):
        if j in (4, 5):
            flat.append(part[0])
        else:
            flat += [part[0], part[1]]
    own, away = run_kernel(
        attend_kernel, where, [keep[:1], q_got] + flat,
        [S((rows, HEAD_DIM), BF16)] * 2, [pltpu.VMEM((128, 16 * rows), F32)], 32,
        8 * rows * 16 * rows * HEAD_DIM, 4 << 20, 2 * rows * 16 * rows)
    back = shift(away, "xl", 1)
    blocks_out = [S((blocks, rows, block), BF16)] * 2
    mine, other = run_kernel(
        project_out_kernel, where, [own, back, out_weight], blocks_out, [], 16,
        2 * rows * block * width, 4 << 20)
    frame_cols = lax.dynamic_slice_in_dim(frames, lax.axis_index(WT) * block, block, 1)
    mixed = (frame_cols.astype(F32) + reduce_features(mine, other)).astype(BF16)
    mine, other = gather_features(mixed)
    gated = run_kernel(
        glu_kernel, where, [mine, other, conv_norm_gain.reshape(1, width), glu_full],
        S((rows, block), BF16), [pltpu.VMEM((2 * blocks, rows, block), BF16)], 24,
        4 * rows * block * width, 6 << 20)
    rim = 16
    before = shift(gated[rows - rim :], SEQ, 1)
    after = shift(gated[:rim], SEQ, -1)
    mine, other = run_kernel(
        conv_kernel, where,
        [gated, before, after, depth_kernel, norm_scale.reshape(1, block), norm_shift.reshape(1, block), conv_weight],
        blocks_out, [pltpu.VMEM((rows + 2 * rim, block), F32), pltpu.VMEM((rows, block), BF16)], 16,
        2 * rows * block * width, 4 << 20)
    return (mixed.astype(F32) + reduce_features(mine, other)).astype(BF16)


def solution(mesh):
    split = Mesh(mesh.devices.reshape(8, 2, 2, 4, 2), ("z", "xl", "xh", "y", "c"))
    in_specs = (
        P(SEQ, None),
        P(),
        P(None, SEQ, WT),
        P(SEQ, WT),
        P(),
        P(None, SEQ, WT),
        P(None, WT),
        P(WT),
        P(WT),
        P(SEQ, WT),
    )
    return jax.shard_map(local, mesh=split, in_specs=in_specs, out_specs=P(SEQ, WT), check_vma=False)
```

```python
import jax
import jax.numpy as jnp
from jax import lax
from jax.experimental import pallas as pl
from jax.experimental.pallas import tpu as pltpu
from jax.sharding import Mesh, PartitionSpec as P

HEAD_DIM = 128
BF16 = jnp.bfloat16
F32 = jnp.float32
SEQ = ("z", "xl")
WT = ("xh", "y", "c")
CHIPS = ("xh", "y")


def shift(value, axis, step):
    count = lax.axis_size(axis)
    return lax.ppermute(value, axis, [(i, (i + step) % count) for i in range(count)])


def smem():
    return pl.BlockSpec(memory_space=pltpu.SMEM)


def vmem():
    return pl.BlockSpec(memory_space=pltpu.VMEM)


def run_kernel(body, where, arrays, outs, scratch, megabytes, flops, moved, exps=0):
    return pl.pallas_call(
        body,
        out_shape=outs,
        in_specs=[smem()] + [vmem()] * len(arrays),
        out_specs=jax.tree.map(lambda _: vmem(), outs),
        scratch_shapes=scratch,
        compiler_params=pltpu.CompilerParams(vmem_limit_bytes=megabytes << 20),
        cost_estimate=pl.CostEstimate(flops=flops, bytes_accessed=moved, transcendentals=exps),
    )(where, *arrays)


def dot(a, b):
    return jnp.dot(a, b, preferred_element_type=F32)


def dot_t(a, b):
    return lax.dot_general(a, b, (((1,), (1,)), ((), ())), preferred_element_type=F32)


def norm_blocks_kernel(where, frames, gain, mine, other):
    rows, width = frames.shape
    blocks = mine.shape[0]
    block = mine.shape[2]
    z, xl, core = where[0], where[1], where[2]
    step_rows = 32

    def chunk(i, carry):
        r = pl.ds(pl.multiple_of(i * step_rows, step_rows), step_rows)
        wide = frames[r, :].astype(F32)
        mean = jnp.mean(wide, axis=-1, keepdims=True)
        centered = wide - mean
        scale = lax.rsqrt(jnp.mean(centered * centered, axis=-1, keepdims=True) + 1e-05)
        for out, first, parity in ((mine, 0, xl), (other, core * other.shape[0], 1 - xl)):
            for j in range(out.shape[0]):
                owner = lax.rem(z + first + j, blocks) * 2 + parity
                cols = pl.ds(pl.multiple_of(owner * block, block), block)
                part = (frames[r, cols].astype(F32) - mean) * scale * gain[:, cols]
                out[j, r, :] = part.astype(BF16)
        return carry

    lax.fori_loop(0, rows // step_rows, chunk, 0)


def project_kernel(where, mine, got, swapped, *refs):
    pieces, (keep, send) = refs[:-2], refs[-2:]
    xl, core = where[1], where[2]
    low = [jnp.where(core == 0, got[j], swapped[j]) for j in range(4)]
    high = [jnp.where(core == 0, swapped[j], got[j]) for j in range(4)]
    for m in range(3):
        for r, a in enumerate((mine, low + high)):
            acc = None
            for j in range(8):
                if j < 4:
                    term = dot(a[j], pieces[j][m])
                elif j == 4:
                    half = pieces[4].shape[1]
                    term = dot(a[4][:, :half], pieces[4][m]) + dot(a[4][:, half:], pieces[5][m])
                else:
                    term = dot(a[j], pieces[j + 1][m])
                acc = term if acc is None else acc + term
            even, odd = acc[:, :HEAD_DIM], acc[:, HEAD_DIM:]
            keep[m, r] = jnp.where(xl == 0, even, odd)
            send[m, r] = jnp.where(xl == 0, odd, even).astype(BF16)


def attend_kernel(where, q_keep, q_got, *refs):
    parts, (mine, send), scores = refs[:-3], refs[-3:-1], refs[-1]
    scale = HEAD_DIM ** (-0.5)
    keys, values = parts[0::2], parts[1::2]
    step_rows = 128
    chunk = keys[0].shape[1] * 2
    for r, out in enumerate((mine, send)):
        for i in range(0, q_keep.shape[2], step_rows):
            query = (q_keep[0, r, i : i + step_rows] + q_got[0, 1 - r, i : i + step_rows].astype(F32)).astype(BF16)
            best = None
            for j, key in enumerate(keys):
                part = dot_t(query, key[...].reshape(chunk, HEAD_DIM))
                scores[:, j * chunk : (j + 1) * chunk] = part
                top = jnp.max(part, axis=-1, keepdims=True)
                best = top if best is None else jnp.maximum(best, top)
            total = jnp.zeros((step_rows, 1), F32)
            acc = jnp.zeros((step_rows, HEAD_DIM), F32)
            for j, value in enumerate(values):
                weights = jnp.exp((scores[:, j * chunk : (j + 1) * chunk] - best) * scale)
                total = total + jnp.sum(weights, axis=-1, keepdims=True)
                acc = acc + dot(weights.astype(BF16), value[...].reshape(chunk, HEAD_DIM))
            out[i : i + step_rows, :] = (acc / total).astype(BF16)


def spread_out(inputs, weight, far_weight, mine, other, same):
    blocks, rows, block = mine.shape
    for j in range(blocks):
        at = slice(j * block, (j + 1) * block)
        a = dot_t(inputs, weight[at, :]).astype(BF16)
        b = dot_t(inputs, far_weight[at, :]).astype(BF16)
        mine[j] = jnp.where(same, a, b)
        other[j] = jnp.where(same, b, a)


def project_out_kernel(where, own, got, weight, far_weight, mine, other):
    xl = where[1]
    a, b = own[...], got[...]
    heads = jnp.concatenate([jnp.where(xl == 0, a, b), jnp.where(xl == 0, b, a)], axis=1)
    spread_out(heads, weight, far_weight, mine, other, where[2] == xl)


def glu_kernel(where, mine, other, gain, weight, far_weight, gated, normed):
    blocks, rows, block = mine.shape
    xl = where[1]
    same = where[2] == xl
    step_rows = 32
    width = 2 * blocks * block

    def chunk(i, carry):
        r = pl.ds(pl.multiple_of(i * step_rows, step_rows), step_rows)
        parts = []
        for j in range(blocks):
            a, b = mine[j, r, :], other[j, r, :]
            parts += [jnp.where(same, a, b).astype(F32), jnp.where(same, b, a).astype(F32)]
        mean = jnp.sum(sum(parts), axis=-1, keepdims=True) / width
        square = sum((p - mean) * (p - mean) for p in parts)
        scale = lax.rsqrt(jnp.sum(square, axis=-1, keepdims=True) / width + 1e-05)
        for n, p in enumerate(parts):
            parity = xl if n % 2 == 0 else 1 - xl
            cols = pl.ds(pl.multiple_of((n // 2 * 2 + parity) * block, block), block)
            normed[n, r, :] = ((p - mean) * scale * gain[:, cols]).astype(BF16)
        return carry

    lax.fori_loop(0, rows // step_rows, chunk, 0)
    sums = [None, None]
    for n in range(2 * blocks):
        source = (weight, far_weight)[n % 2]
        for m in range(2):
            term = dot(normed[n], source[m, n // 2 * block : (n // 2 + 1) * block, :])
            sums[m] = term if sums[m] is None else sums[m] + term
    gated[...] = (sums[0] * jax.nn.sigmoid(sums[1])).astype(BF16)


def conv_kernel(where, gated, before, after, taps, scale, offset, weight, far_weight, mine, other, padded, activated):
    rows = gated.shape[0]
    rim = before.shape[0]
    seq = where[0] * 2 + where[1]
    padded[:rim] = jnp.where(seq > 0, before[...].astype(F32), 0.0)
    padded[rim : rim + rows] = gated[...].astype(F32)
    padded[rim + rows :] = jnp.where(seq < where[3] - 1, after[...].astype(F32), 0.0)
    count = taps.shape[0]
    first = rim - (count - 1) // 2
    for i in range(0, rows, 32):
        acc = None
        for k in range(count):
            term = taps[k : k + 1, :] * padded[i + first + k : i + first + k + 32, :]
            acc = term if acc is None else acc + term
        v = acc * scale[...] + offset[...]
        activated[i : i + 32, :] = (v * jax.nn.sigmoid(v)).astype(BF16)
    spread_out(activated[...], weight, far_weight, mine, other, where[2] == where[1])


def ring(value, first_half, second_half):
    right = left = value
    ahead, behind = [], []
    for _ in range(3):
        right = shift(right, "z", 1)
        left = shift(left, "z", -1)
        ahead.append(left)
        behind.append(right)
    far = [shift(first_half(right), "z", 1), shift(second_half(left), "z", -1)]
    return [value] + ahead + far + behind[::-1]


def reduce_features(mine, other):
    got = shift(other, "c", 1)
    pair = (mine.astype(F32) + got.astype(F32)).astype(BF16)
    parts = lax.all_to_all(pair, CHIPS, 0, 0, tiled=True)
    return jnp.sum(parts.astype(F32), axis=0)


def gather_features(value):
    parts = lax.all_to_all(jnp.broadcast_to(value, (8,) + value.shape), CHIPS, 0, 0, tiled=True)
    return parts, shift(parts, "c", 1)


def local(
    frames,
    attn_norm_gain,
    qkv_weight,
    attn_out_weight,
    conv_norm_gain,
    glu_weight,
    depth_kernel,
    norm_scale,
    norm_shift,
    conv_out_weight,
):
    rows, width = frames.shape
    block = qkv_weight.shape[2]
    blocks = width // block // 2
    z, xl, core = (lax.axis_index(a) for a in ("z", "xl", "c"))
    where = jnp.stack([z, xl, core, lax.axis_size(SEQ)]).astype(jnp.int32)
    S = jax.ShapeDtypeStruct

    out_weight = lax.all_gather(attn_out_weight, "z", axis=0, tiled=True)
    out_weight = [out_weight, shift(out_weight, "xl", 1)]
    glu_half = lax.all_gather(glu_weight, "z", axis=1, tiled=True)
    glu_half = [glu_half, shift(glu_half, "xl", 1)]
    conv_weight = lax.all_gather(conv_out_weight, "z", axis=0, tiled=True)
    conv_weight = [conv_weight, shift(conv_weight, "xl", 1)]

    half = block // 2
    pieces = ring(qkv_weight, lambda v: v[:, :half], lambda v: v[:, half:])
    mine, other = run_kernel(
        norm_blocks_kernel, where, [frames, attn_norm_gain.reshape(1, width)],
        [S((blocks, rows, block), BF16), S((blocks // 2, rows, block), BF16)], [], 16, 10 * rows * width, 4 * rows * width)
    got = shift(other, "xl", 1)
    swapped = shift(got, "c", 1)
    keep, send = run_kernel(
        project_kernel, where, [mine, got, swapped] + pieces,
        [S((3, 2, rows, HEAD_DIM), F32), S((3, 2, rows, HEAD_DIM), BF16)], [], 24,
        6 * rows * width * block, 6 * block * block * 8 + 4 * rows * width)
    kv_got = shift(send[1:], "xl", 1)
    q_got = shift(send[:1], "xl", 1)
    kv = (keep[1:] + kv_got[:, ::-1].astype(F32)).astype(BF16)
    kv_parts = ring(kv, lambda v: v[:1], lambda v: v[1:])
    flat = []
    for j, part in enumerate(kv_parts):
        if j in (4, 5):
            flat.append(part[0])
        else:
            flat += [part[0], part[1]]
    own, away = run_kernel(
        attend_kernel, where, [keep[:1], q_got] + flat,
        [S((rows, HEAD_DIM), BF16)] * 2, [pltpu.VMEM((128, 16 * rows), F32)], 32,
        8 * rows * 16 * rows * HEAD_DIM, 4 << 20, 2 * rows * 16 * rows)
    back = shift(away, "xl", 1)
    blocks_out = [S((blocks, rows, block), BF16)] * 2
    mine, other = run_kernel(
        project_out_kernel, where, [own, back] + out_weight, blocks_out, [], 16,
        2 * rows * block * width, 4 << 20)
    frame_cols = lax.dynamic_slice_in_dim(frames, lax.axis_index(WT) * block, block, 1)
    mixed = (frame_cols.astype(F32) + reduce_features(mine, other)).astype(BF16)
    mine, other = gather_features(mixed)
    gated = run_kernel(
        glu_kernel, where, [mine, other, conv_norm_gain.reshape(1, width)] + glu_half,
        S((rows, block), BF16), [pltpu.VMEM((2 * blocks, rows, block), BF16)], 24,
        4 * rows * block * width, 6 << 20)
    rim = 16
    before = shift(gated[rows - rim :], SEQ, 1)
    after = shift(gated[:rim], SEQ, -1)
    mine, other = run_kernel(
        conv_kernel, where,
        [gated, before, after, depth_kernel, norm_scale.reshape(1, block), norm_shift.reshape(1, block)] + conv_weight,
        blocks_out, [pltpu.VMEM((rows + 2 * rim, block), F32), pltpu.VMEM((rows, block), BF16)], 16,
        2 * rows * block * width, 4 << 20)
    return (mixed.astype(F32) + reduce_features(mine, other)).astype(BF16)


def solution(mesh):
    split = Mesh(mesh.devices.reshape(8, 2, 2, 4, 2), ("z", "xl", "xh", "y", "c"))
    in_specs = (
        P(SEQ, None),
        P(),
        P(None, SEQ, WT),
        P(SEQ, WT),
        P(),
        P(None, SEQ, WT),
        P(None, WT),
        P(WT),
        P(WT),
        P(SEQ, WT),
    )
    return jax.shard_map(local, mesh=split, in_specs=in_specs, out_specs=P(SEQ, WT), check_vma=False)
```

```python
import jax
import jax.numpy as jnp
from jax import lax
from jax.experimental import pallas as pl
from jax.experimental.pallas import tpu as pltpu
from jax.sharding import Mesh, PartitionSpec as P

HEAD_DIM = 128
BF16 = jnp.bfloat16
F32 = jnp.float32
SEQ = ("z", "xl")
WT = ("xh", "y", "c")
CHIPS = ("xh", "y")


def shift(value, axis, step):
    count = lax.axis_size(axis)
    return lax.ppermute(value, axis, [(i, (i + step) % count) for i in range(count)])


def smem():
    return pl.BlockSpec(memory_space=pltpu.SMEM)


def vmem():
    return pl.BlockSpec(memory_space=pltpu.VMEM)


def run_kernel(body, where, arrays, outs, scratch, megabytes, flops, moved, exps=0):
    return pl.pallas_call(
        body,
        out_shape=outs,
        in_specs=[smem()] + [vmem()] * len(arrays),
        out_specs=jax.tree.map(lambda _: vmem(), outs),
        scratch_shapes=scratch,
        compiler_params=pltpu.CompilerParams(vmem_limit_bytes=megabytes << 20),
        cost_estimate=pl.CostEstimate(flops=flops, bytes_accessed=moved, transcendentals=exps),
    )(where, *arrays)


def dot(a, b):
    return jnp.dot(a, b, preferred_element_type=F32)


def dot_t(a, b):
    return lax.dot_general(a, b, (((1,), (1,)), ((), ())), preferred_element_type=F32)


def norm_blocks_kernel(where, frames, gain, mine, other):
    rows, width = frames.shape
    blocks = mine.shape[0]
    block = mine.shape[2]
    z, xl, core = where[0], where[1], where[2]
    step_rows = 32

    def chunk(i, carry):
        r = pl.ds(pl.multiple_of(i * step_rows, step_rows), step_rows)
        wide = frames[r, :].astype(F32)
        mean = jnp.mean(wide, axis=-1, keepdims=True)
        centered = wide - mean
        scale = lax.rsqrt(jnp.mean(centered * centered, axis=-1, keepdims=True) + 1e-05)
        for out, first, parity in ((mine, 0, xl), (other, core * other.shape[0], 1 - xl)):
            for j in range(out.shape[0]):
                owner = lax.rem(z + first + j, blocks) * 2 + parity
                cols = pl.ds(pl.multiple_of(owner * block, block), block)
                part = (frames[r, cols].astype(F32) - mean) * scale * gain[:, cols]
                out[j, r, :] = part.astype(BF16)
        return carry

    lax.fori_loop(0, rows // step_rows, chunk, 0)


def project_kernel(where, mine, got, swapped, *refs):
    pieces, (keep, send) = refs[:-2], refs[-2:]
    xl, core = where[1], where[2]
    low = [jnp.where(core == 0, got[j], swapped[j]) for j in range(4)]
    high = [jnp.where(core == 0, swapped[j], got[j]) for j in range(4)]
    for m in range(3):
        for r, a in enumerate((mine, low + high)):
            acc = None
            for j in range(8):
                if j < 4:
                    term = dot(a[j], pieces[j][m])
                elif j == 4:
                    half = pieces[4].shape[1]
                    term = dot(a[4][:, :half], pieces[4][m]) + dot(a[4][:, half:], pieces[5][m])
                else:
                    term = dot(a[j], pieces[j + 1][m])
                acc = term if acc is None else acc + term
            even, odd = acc[:, :HEAD_DIM], acc[:, HEAD_DIM:]
            keep[m, r] = jnp.where(xl == 0, even, odd)
            send[m, r] = jnp.where(xl == 0, odd, even).astype(BF16)


def attend_kernel(where, q_keep, q_got, *refs):
    parts, (mine, send), scores = refs[:-3], refs[-3:-1], refs[-1]
    scale = HEAD_DIM ** (-0.5)
    keys, values = parts[0::2], parts[1::2]
    step_rows = 128
    chunk = keys[0].shape[1] * 2
    for r, out in enumerate((mine, send)):
        for i in range(0, q_keep.shape[2], step_rows):
            query = (q_keep[0, r, i : i + step_rows] + q_got[0, 1 - r, i : i + step_rows].astype(F32)).astype(BF16)
            best = None
            for j, key in enumerate(keys):
                part = dot_t(query, key[...].reshape(chunk, HEAD_DIM))
                scores[:, j * chunk : (j + 1) * chunk] = part
                top = jnp.max(part, axis=-1, keepdims=True)
                best = top if best is None else jnp.maximum(best, top)
            total = jnp.zeros((step_rows, 1), F32)
            acc = jnp.zeros((step_rows, HEAD_DIM), F32)
            for j, value in enumerate(values):
                weights = jnp.exp((scores[:, j * chunk : (j + 1) * chunk] - best) * scale)
                total = total + jnp.sum(weights, axis=-1, keepdims=True)
                acc = acc + dot(weights.astype(BF16), value[...].reshape(chunk, HEAD_DIM))
            out[i : i + step_rows, :] = (acc / total).astype(BF16)


def spread_out(inputs, pairs, places, mine, other, same):
    for (near, far), place in zip(pairs, places):
        a = dot_t(inputs, near).astype(BF16)
        b = dot_t(inputs, far).astype(BF16)
        mine[place] = jnp.where(same, a, b)
        other[place] = jnp.where(same, b, a)


def project_out_kernel(where, own, got, weight, far_weight, mine, other):
    xl = where[1]
    a, b = own[...], got[...]
    heads = jnp.concatenate([jnp.where(xl == 0, a, b), jnp.where(xl == 0, b, a)], axis=1)
    blocks, rows, block = mine.shape
    pairs = [(weight[j * block : (j + 1) * block], far_weight[j * block : (j + 1) * block]) for j in range(blocks)]
    spread_out(heads, pairs, range(blocks), mine, other, where[2] == xl)


def glu_kernel(where, mine, other, gain, *refs):
    pieces, (gated, normed) = refs[:-2], refs[-2:]
    blocks, rows, block = mine.shape
    z, xl = where[0], where[1]
    same = where[2] == xl
    step_rows = 32
    width = 2 * blocks * block

    def chunk(i, carry):
        r = pl.ds(pl.multiple_of(i * step_rows, step_rows), step_rows)
        parts = []
        for j in range(blocks):
            at = lax.rem(z + j, blocks)
            a, b = mine[at, r, :], other[at, r, :]
            parts += [jnp.where(same, a, b).astype(F32), jnp.where(same, b, a).astype(F32)]
        mean = jnp.sum(sum(parts), axis=-1, keepdims=True) / width
        square = sum((p - mean) * (p - mean) for p in parts)
        scale = lax.rsqrt(jnp.sum(square, axis=-1, keepdims=True) / width + 1e-05)
        for n, p in enumerate(parts):
            parity = xl if n % 2 == 0 else 1 - xl
            cols = pl.ds(pl.multiple_of((lax.rem(z + n // 2, blocks) * 2 + parity) * block, block), block)
            normed[n, r, :] = ((p - mean) * scale * gain[:, cols]).astype(BF16)
        return carry

    lax.fori_loop(0, rows // step_rows, chunk, 0)
    sums = [None, None]
    for n in range(2 * blocks):
        j = n // 2
        for m in range(2):
            if j == 4:
                weight = pieces[4 + m][n % 2]
            else:
                weight = pieces[j if j < 4 else j + 1][2 * m + n % 2]
            term = dot(normed[n], weight)
            sums[m] = term if sums[m] is None else sums[m] + term
    gated[...] = (sums[0] * jax.nn.sigmoid(sums[1])).astype(BF16)


def conv_kernel(where, gated, before, after, taps, scale, offset, *refs):
    pieces, (mine, other, padded, activated) = refs[:-4], refs[-4:]
    rows = gated.shape[0]
    rim = before.shape[0]
    seq = where[0] * 2 + where[1]
    padded[:rim] = jnp.where(seq > 0, before[...].astype(F32), 0.0)
    padded[rim : rim + rows] = gated[...].astype(F32)
    padded[rim + rows :] = jnp.where(seq < where[3] - 1, after[...].astype(F32), 0.0)
    count = taps.shape[0]
    first = rim - (count - 1) // 2
    for i in range(0, rows, 32):
        acc = None
        for k in range(count):
            term = taps[k : k + 1, :] * padded[i + first + k : i + first + k + 32, :]
            acc = term if acc is None else acc + term
        v = acc * scale[...] + offset[...]
        activated[i : i + 32, :] = (v * jax.nn.sigmoid(v)).astype(BF16)
    pairs = [(pieces[4][0], pieces[5][0]) if j == 4 else (pieces[j if j < 4 else j + 1][4], pieces[j if j < 4 else j + 1][5]) for j in range(8)]
    places = [lax.rem(where[0] + j, 8) for j in range(8)]
    spread_out(activated[...], pairs, places, mine, other, where[2] == where[1])


def ring(value, first_half, second_half):
    right = left = value
    ahead, behind = [], []
    for _ in range(3):
        right = shift(right, "z", 1)
        left = shift(left, "z", -1)
        ahead.append(left)
        behind.append(right)
    far = [shift(first_half(right), "z", 1), shift(second_half(left), "z", -1)]
    return [value] + ahead + far + behind[::-1]


def pair_sum(mine, other):
    got = shift(other, "c", 1)
    return (mine.astype(F32) + got.astype(F32)).astype(BF16)


def reduce_features(pair):
    parts = lax.all_to_all(pair, CHIPS, 0, 0, tiled=True)
    return jnp.sum(parts.astype(F32), axis=0)


def gather_features(value):
    parts = lax.all_to_all(jnp.broadcast_to(value, (8,) + value.shape), CHIPS, 0, 0, tiled=True)
    return parts, shift(parts, "c", 1)


def local(
    frames,
    attn_norm_gain,
    qkv_weight,
    attn_out_weight,
    conv_norm_gain,
    glu_weight,
    depth_kernel,
    norm_scale,
    norm_shift,
    conv_out_weight,
):
    rows, width = frames.shape
    block = qkv_weight.shape[2]
    blocks = width // block // 2
    z, xl, core = (lax.axis_index(a) for a in ("z", "xl", "c"))
    where = jnp.stack([z, xl, core, lax.axis_size(SEQ)]).astype(jnp.int32)
    S = jax.ShapeDtypeStruct

    out_weight = lax.all_gather(attn_out_weight, "z", axis=0, tiled=True)
    out_weight = [out_weight, shift(out_weight, "xl", 1)]
    late = jnp.concatenate([glu_weight, conv_out_weight[None]])
    late_far = shift(late, "xl", 1)

    half = block // 2
    pieces = ring(qkv_weight, lambda v: v[:, :half], lambda v: v[:, half:])
    mine, other = run_kernel(
        norm_blocks_kernel, where, [frames, attn_norm_gain.reshape(1, width)],
        [S((blocks, rows, block), BF16), S((blocks // 2, rows, block), BF16)], [], 16, 10 * rows * width, 4 * rows * width)
    got = shift(other, "xl", 1)
    swapped, late_far = lax.optimization_barrier((shift(got, "c", 1), late_far))
    late = jnp.stack([late, late_far], axis=1).reshape(6, block, block)
    keep, send = run_kernel(
        project_kernel, where, [mine, got, swapped] + pieces,
        [S((3, 2, rows, HEAD_DIM), F32), S((3, 2, rows, HEAD_DIM), BF16)], [], 24,
        6 * rows * width * block, 6 * block * block * 8 + 4 * rows * width)
    kv_got = shift(send[1:], "xl", 1)
    q_got = shift(send[:1], "xl", 1)
    kv = (keep[1:] + kv_got[:, ::-1].astype(F32)).astype(BF16)
    kv_parts = ring(kv, lambda v: v[:1], lambda v: v[1:])
    late, kv_parts[3], kv_parts[6] = lax.optimization_barrier((late, kv_parts[3], kv_parts[6]))
    right1, left1 = shift(late, "z", 1), shift(late, "z", -1)
    flat = []
    for j, part in enumerate(kv_parts):
        if j in (4, 5):
            flat.append(part[0])
        else:
            flat += [part[0], part[1]]
    own, away = run_kernel(
        attend_kernel, where, [keep[:1], q_got] + flat,
        [S((rows, HEAD_DIM), BF16)] * 2, [pltpu.VMEM((128, 16 * rows), F32)], 32,
        8 * rows * 16 * rows * HEAD_DIM, 4 << 20, 2 * rows * 16 * rows)
    back, right1, left1 = lax.optimization_barrier((shift(away, "xl", 1), right1, left1))
    blocks_out = [S((blocks, rows, block), BF16)] * 2
    mine, other = run_kernel(
        project_out_kernel, where, [own, back] + out_weight, blocks_out, [], 16,
        2 * rows * block * width, 4 << 20)
    frame_cols = lax.dynamic_slice_in_dim(frames, lax.axis_index(WT) * block, block, 1)
    right2, left2 = shift(right1, "z", 1), shift(left1, "z", -1)
    pair = pair_sum(mine, other)
    mixed = (frame_cols.astype(F32) + reduce_features(pair)).astype(BF16)
    ready, right2, left2 = lax.optimization_barrier((mixed, right2, left2))
    right3, left3 = shift(right2, "z", 1), shift(left2, "z", -1)
    mine, other = gather_features(ready)
    far = [shift(right3[:2], "z", 1), shift(left3[2:4], "z", -1)]
    last = [shift(right3[4:5], "z", 1), shift(left3[5:], "z", -1)]
    near, behind = [late, left1, left2, left3], [right3, right2, right1]
    gated = run_kernel(
        glu_kernel, where, [mine, other, conv_norm_gain.reshape(1, width)] + near + far + behind,
        S((rows, block), BF16), [pltpu.VMEM((2 * blocks, rows, block), BF16)], 24,
        4 * rows * block * width, 6 << 20)
    rim = 16
    before = shift(gated[rows - rim :], SEQ, 1)
    after = shift(gated[:rim], SEQ, -1)
    mine, other = run_kernel(
        conv_kernel, where,
        [gated, before, after, depth_kernel, norm_scale.reshape(1, block), norm_shift.reshape(1, block)] + near + last + behind,
        blocks_out, [pltpu.VMEM((rows + 2 * rim, block), F32), pltpu.VMEM((rows, block), BF16)], 16,
        2 * rows * block * width, 4 << 20)
    return (mixed.astype(F32) + reduce_features(pair_sum(mine, other))).astype(BF16)


def solution(mesh):
    split = Mesh(mesh.devices.reshape(8, 2, 2, 4, 2), ("z", "xl", "xh", "y", "c"))
    in_specs = (
        P(SEQ, None),
        P(),
        P(None, SEQ, WT),
        P(SEQ, WT),
        P(),
        P(None, SEQ, WT),
        P(None, WT),
        P(WT),
        P(WT),
        P(SEQ, WT),
    )
    return jax.shard_map(local, mesh=split, in_specs=in_specs, out_specs=P(SEQ, WT), check_vma=False)
```

```python
import jax
import jax.numpy as jnp
from jax import lax
from jax.experimental import pallas as pl
from jax.experimental.pallas import tpu as pltpu
from jax.sharding import Mesh, PartitionSpec as P

HEAD_DIM = 128
BF16 = jnp.bfloat16
F32 = jnp.float32
SEQ = ("z", "xl")
WT = ("xh", "y", "c")
CHIPS = ("xh", "y")


def shift(value, axis, step):
    count = lax.axis_size(axis)
    return lax.ppermute(value, axis, [(i, (i + step) % count) for i in range(count)])


def smem():
    return pl.BlockSpec(memory_space=pltpu.SMEM)


def vmem():
    return pl.BlockSpec(memory_space=pltpu.VMEM)


def run_kernel(body, where, arrays, outs, scratch, megabytes, flops, moved, exps=0):
    return pl.pallas_call(
        body,
        out_shape=outs,
        in_specs=[smem()] + [vmem()] * len(arrays),
        out_specs=jax.tree.map(lambda _: vmem(), outs),
        scratch_shapes=scratch,
        compiler_params=pltpu.CompilerParams(vmem_limit_bytes=megabytes << 20),
        cost_estimate=pl.CostEstimate(flops=flops, bytes_accessed=moved, transcendentals=exps),
    )(where, *arrays)


def dot(a, b):
    return jnp.dot(a, b, preferred_element_type=F32)


def dot_t(a, b):
    return lax.dot_general(a, b, (((1,), (1,)), ((), ())), preferred_element_type=F32)


def norm_blocks_kernel(where, frames, gain, mine, other):
    rows, width = frames.shape
    blocks = mine.shape[0]
    block = mine.shape[2]
    z, xl, core = where[0], where[1], where[2]
    step_rows = 32

    def chunk(i, carry):
        r = pl.ds(pl.multiple_of(i * step_rows, step_rows), step_rows)
        wide = frames[r, :].astype(F32)
        mean = jnp.mean(wide, axis=-1, keepdims=True)
        centered = wide - mean
        scale = lax.rsqrt(jnp.mean(centered * centered, axis=-1, keepdims=True) + 1e-05)
        for out, first, parity in ((mine, 0, xl), (other, core * other.shape[0], 1 - xl)):
            for j in range(out.shape[0]):
                owner = lax.rem(z + first + j, blocks) * 2 + parity
                cols = pl.ds(pl.multiple_of(owner * block, block), block)
                part = (frames[r, cols].astype(F32) - mean) * scale * gain[:, cols]
                out[j, r, :] = part.astype(BF16)
        return carry

    lax.fori_loop(0, rows // step_rows, chunk, 0)


def project_kernel(where, mine, got, swapped, *refs):
    pieces, (keep, send) = refs[:-2], refs[-2:]
    xl, core = where[1], where[2]
    low = [jnp.where(core == 0, got[j], swapped[j]) for j in range(4)]
    high = [jnp.where(core == 0, swapped[j], got[j]) for j in range(4)]
    count = keep.shape[0]
    for m in range(count):
        for r, a in enumerate((mine, low + high)):
            acc = None
            for j in range(8):
                if count == 1 or j < 4:
                    weight = pieces[j][m]
                else:
                    weight = pieces[4 + m][0] if j == 4 else pieces[j + 1][m]
                term = dot(a[j], weight)
                acc = term if acc is None else acc + term
            even, odd = acc[:, :HEAD_DIM], acc[:, HEAD_DIM:]
            keep[m, r] = jnp.where(xl == 0, even, odd)
            send[m, r] = jnp.where(xl == 0, odd, even).astype(BF16)


def attend_kernel(where, q_keep, q_got, *refs):
    parts, (mine, send), scores = refs[:-3], refs[-3:-1], refs[-1]
    scale = HEAD_DIM ** (-0.5)
    keys, values = parts[0::2], parts[1::2]
    step_rows = 128
    chunk = keys[0].shape[1] * 2
    for r, out in enumerate((mine, send)):
        for i in range(0, q_keep.shape[2], step_rows):
            query = (q_keep[0, r, i : i + step_rows] + q_got[0, 1 - r, i : i + step_rows].astype(F32)).astype(BF16)
            best = None
            for j, key in enumerate(keys):
                part = dot_t(query, key[...].reshape(chunk, HEAD_DIM))
                scores[:, j * chunk : (j + 1) * chunk] = part
                top = jnp.max(part, axis=-1, keepdims=True)
                best = top if best is None else jnp.maximum(best, top)
            total = jnp.zeros((step_rows, 1), F32)
            acc = jnp.zeros((step_rows, HEAD_DIM), F32)
            for j, value in enumerate(values):
                weights = jnp.exp((scores[:, j * chunk : (j + 1) * chunk] - best) * scale)
                total = total + jnp.sum(weights, axis=-1, keepdims=True)
                acc = acc + dot(weights.astype(BF16), value[...].reshape(chunk, HEAD_DIM))
            out[i : i + step_rows, :] = (acc / total).astype(BF16)


def spread_out(inputs, pairs, mine, other, same):
    for j, (near, far) in enumerate(pairs):
        a = dot_t(inputs, near).astype(BF16)
        b = dot_t(inputs, far).astype(BF16)
        mine[j] = jnp.where(same, a, b)
        other[j] = jnp.where(same, b, a)


def project_out_kernel(where, own, got, weight, far_weight, mine, other):
    xl = where[1]
    a, b = own[...], got[...]
    heads = jnp.concatenate([jnp.where(xl == 0, a, b), jnp.where(xl == 0, b, a)], axis=1)
    blocks, rows, block = mine.shape
    pairs = [(weight[j * block : (j + 1) * block], far_weight[j * block : (j + 1) * block]) for j in range(blocks)]
    spread_out(heads, pairs, mine, other, where[2] == xl)


def glu_kernel(where, mine, other, gain, *refs):
    pieces, (gated, normed) = refs[:-2], refs[-2:]
    blocks, rows, block = mine.shape
    z, xl = where[0], where[1]
    same = where[2] == xl
    step_rows = 32
    width = 2 * blocks * block

    def chunk(i, carry):
        r = pl.ds(pl.multiple_of(i * step_rows, step_rows), step_rows)
        parts = []
        for j in range(blocks):
            at = lax.rem(z + j, blocks)
            a, b = mine[at, r, :], other[at, r, :]
            parts += [jnp.where(same, a, b).astype(F32), jnp.where(same, b, a).astype(F32)]
        mean = jnp.sum(sum(parts), axis=-1, keepdims=True) / width
        square = sum((p - mean) * (p - mean) for p in parts)
        scale = lax.rsqrt(jnp.sum(square, axis=-1, keepdims=True) / width + 1e-05)
        for n, p in enumerate(parts):
            parity = xl if n % 2 == 0 else 1 - xl
            cols = pl.ds(pl.multiple_of((lax.rem(z + n // 2, blocks) * 2 + parity) * block, block), block)
            normed[n, r, :] = ((p - mean) * scale * gain[:, cols]).astype(BF16)
        return carry

    lax.fori_loop(0, rows // step_rows, chunk, 0)
    sums = [None, None]
    for n in range(2 * blocks):
        j = n // 2
        for m in range(2):
            if j == 4:
                weight = pieces[4 + m][n % 2]
            else:
                weight = pieces[j if j < 4 else j + 1][2 * m + n % 2]
            term = dot(normed[n], weight)
            sums[m] = term if sums[m] is None else sums[m] + term
    gated[...] = (sums[0] * jax.nn.sigmoid(sums[1])).astype(BF16)


def conv_kernel(where, gated, before, after, taps, scale, offset, weight, mine, other, padded, activated):
    rows = gated.shape[0]
    rim = before.shape[0]
    seq = where[0] * 2 + where[1]
    padded[:rim] = jnp.where(seq > 0, before[...].astype(F32), 0.0)
    padded[rim : rim + rows] = gated[...].astype(F32)
    padded[rim + rows :] = jnp.where(seq < where[3] - 1, after[...].astype(F32), 0.0)
    count = taps.shape[0]
    first = rim - (count - 1) // 2
    for i in range(0, rows, 32):
        acc = None
        for k in range(count):
            term = taps[k : k + 1, :] * padded[i + first + k : i + first + k + 32, :]
            acc = term if acc is None else acc + term
        v = acc * scale[...] + offset[...]
        activated[i : i + 32, :] = (v * jax.nn.sigmoid(v)).astype(BF16)
    pairs = [(weight[j, 0], weight[j, 1]) for j in range(weight.shape[0])]
    spread_out(activated[...], pairs, mine, other, where[2] == where[1])


def both_ways(right, left):
    return shift(right, "z", 1), shift(left, "z", -1)


def pair_sum(mine, other):
    got = shift(other, "c", 1)
    return (mine.astype(F32) + got.astype(F32)).astype(BF16)


def reduce_features(pair):
    parts = lax.all_to_all(pair, CHIPS, 0, 0, tiled=True)
    return jnp.sum(parts.astype(F32), axis=0)


def gather_features(value):
    return lax.all_to_all(jnp.broadcast_to(value, (8,) + value.shape), CHIPS, 0, 0, tiled=True)


def local(
    frames,
    attn_norm_gain,
    qkv_weight,
    attn_out_weight,
    conv_norm_gain,
    glu_weight,
    depth_kernel,
    norm_scale,
    norm_shift,
    conv_out_weight,
):
    rows, width = frames.shape
    block = qkv_weight.shape[2]
    blocks = width // block // 2
    z, xl, core = (lax.axis_index(a) for a in ("z", "xl", "c"))
    where = jnp.stack([z, xl, core, lax.axis_size(SEQ)]).astype(jnp.int32)
    S = jax.ShapeDtypeStruct

    def project(pieces, count):
        shape = (count, 2, rows, HEAD_DIM)
        return run_kernel(
            project_kernel, where, [mine, got, swapped] + pieces, [S(shape, F32), S(shape, BF16)], [], 20,
            2 * count * rows * width * block, 2 * count * block * block * 8 + 4 * rows * width)

    step = lax.optimization_barrier
    out_weight = lax.all_gather(attn_out_weight, "z", axis=0, tiled=True)
    late = jnp.concatenate([glu_weight, conv_out_weight[None]])
    late_far = shift(late, "xl", 1)
    kv_weight = qkv_weight[1:]

    r1, l1 = both_ways(kv_weight, kv_weight)
    mine, other = run_kernel(
        norm_blocks_kernel, where, [frames, attn_norm_gain.reshape(1, width)],
        [S((blocks, rows, block), BF16), S((blocks // 2, rows, block), BF16)], [], 16, 10 * rows * width, 4 * rows * width)
    r1, l1, other = step((r1, l1, other))

    r2, l2 = both_ways(r1, l1)
    got = shift(other, "xl", 1)
    r2, l2, got = step((r2, l2, got))

    r3, l3 = both_ways(r2, l2)
    swapped = shift(got, "c", 1)
    r3, l3, swapped, late_far, q_weight = step((r3, l3, swapped, late_far, qkv_weight[:1]))
    late = jnp.stack([late, late_far], axis=1)
    conv_weight, late = late[2], late[:2].reshape(4, block, block)

    far_k, far_v = both_ways(r3[:1], l3[1:])
    q_r1, q_l1 = both_ways(q_weight, q_weight)
    far_k, far_v, q_r1, q_l1, late = step((far_k, far_v, q_r1, q_l1, late))

    q_r2, q_l2 = both_ways(q_r1, q_l1)
    late_r1, late_l1 = both_ways(late, late)
    keep, send = project([kv_weight, l1, l2, l3, far_k, far_v, r3, r2, r1], 2)
    kv_got, q_r2, q_l2 = step((shift(send, "xl", 1), q_r2, q_l2))

    kv = (keep + kv_got[:, ::-1].astype(F32)).astype(BF16)
    kv_r1, kv_l1 = both_ways(kv, kv)
    q_r3, q_l3 = both_ways(q_r2, q_l2)
    kv_r1, kv_l1, q_r3, q_l3, late_r1, late_l1 = step((kv_r1, kv_l1, q_r3, q_l3, late_r1, late_l1))

    kv_r2, kv_l2 = both_ways(kv_r1, kv_l1)
    q_far = shift(q_r3, "z", 1)
    kv_r2, kv_l2, q_far, out_weight = step((kv_r2, kv_l2, q_far, out_weight))

    kv_r3, kv_l3 = both_ways(kv_r2, kv_l2)
    out_weight = [out_weight, shift(out_weight, "xl", 1)]
    q_keep, q_send = project([q_weight, q_l1, q_l2, q_l3, q_far, q_r3, q_r2, q_r1], 1)
    kv_r3, kv_l3, q_got = step((kv_r3, kv_l3, shift(q_send, "xl", 1)))

    far_k, far_v = both_ways(kv_r3[:1], kv_l3[1:])
    far_k, far_v, late_r1, late_l1, conv_weight = step((far_k, far_v, late_r1, late_l1, conv_weight))
    conv_weight = lax.all_gather(conv_weight, "z", axis=0)

    late_r2, late_l2 = both_ways(late_r1, late_l1)
    flat = []
    for part in (kv, kv_l1, kv_l2, kv_l3):
        flat += [part[0], part[1]]
    flat += [far_k[0], far_v[0]]
    for part in (kv_r3, kv_r2, kv_r1):
        flat += [part[0], part[1]]
    own, away = run_kernel(
        attend_kernel, where, [q_keep, q_got] + flat,
        [S((rows, HEAD_DIM), BF16)] * 2, [pltpu.VMEM((128, 16 * rows), F32)], 32,
        8 * rows * 16 * rows * HEAD_DIM, 4 << 20, 2 * rows * 16 * rows)
    back, late_r2, late_l2 = step((shift(away, "xl", 1), late_r2, late_l2))

    late_r3, late_l3 = both_ways(late_r2, late_l2)
    blocks_out = [S((blocks, rows, block), BF16)] * 2
    mine, other = run_kernel(
        project_out_kernel, where, [own, back] + out_weight, blocks_out, [], 16,
        2 * rows * block * width, 4 << 20)
    share = reduce_features(pair_sum(mine, other))
    frame_cols = lax.dynamic_slice_in_dim(frames, lax.axis_index(WT) * block, block, 1)
    mixed = (frame_cols.astype(F32) + share).astype(BF16)
    ready, late_r3, late_l3 = step((mixed, late_r3, late_l3))

    late_far = both_ways(late_r3[:2], late_l3[2:])
    mine, *late_far = step((gather_features(ready), *late_far))
    other = shift(mine, "c", 1)
    late = [late, late_l1, late_l2, late_l3, *late_far, late_r3, late_r2, late_r1]
    gated = run_kernel(
        glu_kernel, where, [mine, other, conv_norm_gain.reshape(1, width)] + late,
        S((rows, block), BF16), [pltpu.VMEM((2 * blocks, rows, block), BF16)], 24,
        4 * rows * block * width, 6 << 20)
    rim = 16
    before = shift(gated[rows - rim :], SEQ, 1)
    after = shift(gated[:rim], SEQ, -1)
    mine, other = run_kernel(
        conv_kernel, where,
        [gated, before, after, depth_kernel, norm_scale.reshape(1, block), norm_shift.reshape(1, block), conv_weight],
        blocks_out, [pltpu.VMEM((rows + 2 * rim, block), F32), pltpu.VMEM((rows, block), BF16)], 16,
        2 * rows * block * width, 4 << 20)
    return (mixed.astype(F32) + reduce_features(pair_sum(mine, other))).astype(BF16)


def solution(mesh):
    split = Mesh(mesh.devices.reshape(8, 2, 2, 4, 2), ("z", "xl", "xh", "y", "c"))
    in_specs = (
        P(SEQ, None),
        P(),
        P(None, SEQ, WT),
        P(SEQ, WT),
        P(),
        P(None, SEQ, WT),
        P(None, WT),
        P(WT),
        P(WT),
        P(SEQ, WT),
    )
    return jax.shard_map(local, mesh=split, in_specs=in_specs, out_specs=P(SEQ, WT), check_vma=False)
```

```python
import jax
import jax.numpy as jnp
from jax import lax
from jax.experimental import pallas as pl
from jax.experimental.pallas import tpu as pltpu
from jax.sharding import Mesh, PartitionSpec as P

HEAD_DIM = 128
BF16 = jnp.bfloat16
F32 = jnp.float32
SEQ = ("z", "xl")
WT = ("xh", "y", "c")
CHIPS = ("xh", "y")


def shift(value, axis, step):
    count = lax.axis_size(axis)
    return lax.ppermute(value, axis, [(i, (i + step) % count) for i in range(count)])


def smem():
    return pl.BlockSpec(memory_space=pltpu.SMEM)


def vmem():
    return pl.BlockSpec(memory_space=pltpu.VMEM)


def run_kernel(body, where, arrays, outs, scratch, megabytes, flops, moved, exps=0):
    return pl.pallas_call(
        body,
        out_shape=outs,
        in_specs=[smem()] + [vmem()] * len(arrays),
        out_specs=jax.tree.map(lambda _: vmem(), outs),
        scratch_shapes=scratch,
        compiler_params=pltpu.CompilerParams(vmem_limit_bytes=60 << 20),
        cost_estimate=pl.CostEstimate(flops=flops, bytes_accessed=moved, transcendentals=exps),
    )(where, *arrays)


def dot(a, b):
    return jnp.dot(a, b, preferred_element_type=F32)


def dot_t(a, b):
    return lax.dot_general(a, b, (((1,), (1,)), ((), ())), preferred_element_type=F32)


def norm_blocks_kernel(where, frames, gain, mine, other):
    rows, width = frames.shape
    blocks = mine.shape[0]
    block = mine.shape[2]
    z, xl, core = where[0], where[1], where[2]
    step_rows = 32

    def chunk(i, carry):
        r = pl.ds(pl.multiple_of(i * step_rows, step_rows), step_rows)
        wide = frames[r, :].astype(F32)
        mean = jnp.mean(wide, axis=-1, keepdims=True)
        centered = wide - mean
        scale = lax.rsqrt(jnp.mean(centered * centered, axis=-1, keepdims=True) + 1e-05)
        for out, first, parity in ((mine, 0, xl), (other, core * other.shape[0], 1 - xl)):
            for j in range(out.shape[0]):
                owner = lax.rem(z + first + j, blocks) * 2 + parity
                cols = pl.ds(pl.multiple_of(owner * block, block), block)
                part = (frames[r, cols].astype(F32) - mean) * scale * gain[:, cols]
                out[j, r, :] = part.astype(BF16)
        return carry

    lax.fori_loop(0, rows // step_rows, chunk, 0)


def project_kernel(where, mine, got, swapped, *refs):
    pieces, (kv_keep, kv_send, q_keep, q_send) = refs[:-4], refs[-4:]
    xl, core = where[1], where[2]
    low = [jnp.where(core == 0, got[j], swapped[j]) for j in range(4)]
    high = [jnp.where(core == 0, swapped[j], got[j]) for j in range(4)]
    half = pieces[4].shape[1]
    for m, keep, send, at in ((0, q_keep, q_send, 0), (1, kv_keep, kv_send, 0), (2, kv_keep, kv_send, 1)):
        for r, a in enumerate((mine, low + high)):
            acc = None
            for j in range(8):
                if j == 4:
                    term = dot(a[j][:, :half], pieces[4][m]) + dot(a[j][:, half:], pieces[5][m])
                else:
                    term = dot(a[j], pieces[j if j < 4 else j + 1][m])
                acc = term if acc is None else acc + term
            even, odd = acc[:, :HEAD_DIM], acc[:, HEAD_DIM:]
            keep[at, r] = jnp.where(xl == 0, even, odd)
            send[at, r] = jnp.where(xl == 0, odd, even).astype(BF16)


def attend_kernel(where, q_keep, q_got, *refs):
    parts, (mine, send), scores = refs[:-3], refs[-3:-1], refs[-1]
    scale = HEAD_DIM ** (-0.5)
    step_rows = 128
    chunk = parts[0].shape[1] * parts[0].shape[2]
    count = len(parts) - 1

    def piece(j, side):
        whole = parts[j][side] if j < count - 1 else parts[j + side][0]
        return whole.reshape(chunk, HEAD_DIM)

    for r, out in enumerate((mine, send)):
        for i in range(0, q_keep.shape[2], step_rows):
            query = (q_keep[0, r, i : i + step_rows] + q_got[0, 1 - r, i : i + step_rows].astype(F32)).astype(BF16)
            best = None
            for j in range(count):
                part = dot_t(query, piece(j, 0))
                scores[:, j * chunk : (j + 1) * chunk] = part
                top = jnp.max(part, axis=-1, keepdims=True)
                best = top if best is None else jnp.maximum(best, top)
            total = jnp.zeros((step_rows, 1), F32)
            acc = jnp.zeros((step_rows, HEAD_DIM), F32)
            for j in range(count):
                weights = jnp.exp((scores[:, j * chunk : (j + 1) * chunk] - best) * scale)
                total = total + jnp.sum(weights, axis=-1, keepdims=True)
                acc = acc + dot(weights.astype(BF16), piece(j, 1))
            out[i : i + step_rows, :] = (acc / total).astype(BF16)


def spread_out(inputs, pairs, mine, other, same):
    for j, (near, far) in enumerate(pairs):
        a = dot_t(inputs, near).astype(BF16)
        b = dot_t(inputs, far).astype(BF16)
        mine[j] = jnp.where(same, a, b)
        other[j] = jnp.where(same, b, a)


def project_out_kernel(where, own, got, weight, far_weight, mine, other):
    xl = where[1]
    a, b = own[...], got[...]
    heads = jnp.concatenate([jnp.where(xl == 0, a, b), jnp.where(xl == 0, b, a)], axis=1)
    blocks, rows, block = mine.shape
    pairs = [(weight[j * block : (j + 1) * block], far_weight[j * block : (j + 1) * block]) for j in range(blocks)]
    spread_out(heads, pairs, mine, other, where[2] == xl)


def glu_kernel(where, mine, other, gain, *refs):
    pieces, (gated, normed) = refs[:-2], refs[-2:]
    blocks, rows, block = mine.shape
    z, xl = where[0], where[1]
    same = where[2] == xl
    step_rows = 32
    width = 2 * blocks * block

    def chunk(i, carry):
        r = pl.ds(pl.multiple_of(i * step_rows, step_rows), step_rows)
        parts = []
        for j in range(blocks):
            at = lax.rem(z + j, blocks)
            a, b = mine[at, r, :], other[at, r, :]
            parts += [jnp.where(same, a, b).astype(F32), jnp.where(same, b, a).astype(F32)]
        mean = jnp.sum(sum(parts), axis=-1, keepdims=True) / width
        square = sum((p - mean) * (p - mean) for p in parts)
        scale = lax.rsqrt(jnp.sum(square, axis=-1, keepdims=True) / width + 1e-05)
        for n, p in enumerate(parts):
            parity = xl if n % 2 == 0 else 1 - xl
            cols = pl.ds(pl.multiple_of((lax.rem(z + n // 2, blocks) * 2 + parity) * block, block), block)
            normed[n, r, :] = ((p - mean) * scale * gain[:, cols]).astype(BF16)
        return carry

    lax.fori_loop(0, rows // step_rows, chunk, 0)
    sums = [None, None]
    for n in range(2 * blocks):
        j = n // 2
        for m in range(2):
            if j == 4:
                weight = pieces[4 + m][n % 2]
            else:
                weight = pieces[j if j < 4 else j + 1][2 * m + n % 2]
            term = dot(normed[n], weight)
            sums[m] = term if sums[m] is None else sums[m] + term
    gated[...] = (sums[0] * jax.nn.sigmoid(sums[1])).astype(BF16)


def conv_kernel(where, gated, before, after, taps, scale, offset, weight, mine, other, padded, activated):
    rows = gated.shape[0]
    rim = before.shape[0]
    seq = where[0] * 2 + where[1]
    padded[:rim] = jnp.where(seq > 0, before[...].astype(F32), 0.0)
    padded[rim : rim + rows] = gated[...].astype(F32)
    padded[rim + rows :] = jnp.where(seq < where[3] - 1, after[...].astype(F32), 0.0)
    count = taps.shape[0]
    first = rim - (count - 1) // 2
    for i in range(0, rows, 32):
        acc = None
        for k in range(count):
            term = taps[k : k + 1, :] * padded[i + first + k : i + first + k + 32, :]
            acc = term if acc is None else acc + term
        v = acc * scale[...] + offset[...]
        activated[i : i + 32, :] = (v * jax.nn.sigmoid(v)).astype(BF16)
    pairs = [(weight[j, 0], weight[j, 1]) for j in range(weight.shape[0])]
    spread_out(activated[...], pairs, mine, other, where[2] == where[1])


def both_ways(right, left):
    return shift(right, "z", 1), shift(left, "z", -1)


def pair_sum(mine, other):
    got = shift(other, "c", 1)
    return (mine.astype(F32) + got.astype(F32)).astype(BF16)


def reduce_features(pair):
    parts = lax.all_to_all(pair, CHIPS, 0, 0, tiled=True)
    return jnp.sum(parts.astype(F32), axis=0)


def gather_features(value):
    return lax.all_to_all(jnp.broadcast_to(value, (8,) + value.shape), CHIPS, 0, 0, tiled=True)


def local(
    frames,
    attn_norm_gain,
    qkv_weight,
    attn_out_weight,
    conv_norm_gain,
    glu_weight,
    depth_kernel,
    norm_scale,
    norm_shift,
    conv_out_weight,
):
    rows, width = frames.shape
    block = qkv_weight.shape[2]
    blocks = width // block // 2
    z, xl, core = (lax.axis_index(a) for a in ("z", "xl", "c"))
    where = jnp.stack([z, xl, core, lax.axis_size(SEQ)]).astype(jnp.int32)
    S = jax.ShapeDtypeStruct

    step = lax.optimization_barrier
    out_weight = lax.all_gather(attn_out_weight, "z", axis=0, tiled=True)
    late = jnp.concatenate([glu_weight, conv_out_weight[None]])
    late_far = shift(late, "xl", 1)

    half = block // 2
    r1, l1 = both_ways(qkv_weight, qkv_weight)
    mine, other = run_kernel(
        norm_blocks_kernel, where, [frames, attn_norm_gain.reshape(1, width)],
        [S((blocks, rows, block), BF16), S((blocks // 2, rows, block), BF16)], [], 12, 10 * rows * width, 4 * rows * width)
    got = shift(other, "xl", 1)
    r2, l2 = both_ways(r1, l1)
    r3, l3 = both_ways(r2, l2)
    far = both_ways(r3[:, :half], l3[:, half:])
    swapped, late_far = step((shift(got, "c", 1), late_far))
    late = jnp.stack([late, late_far], axis=1)
    conv_weight, late = late[2], late[:2].reshape(4, block, block)

    late, r3, l3 = step((late, r3, l3))
    late_r1, late_l1 = both_ways(late, late)
    shapes = [(2, 2, rows, HEAD_DIM), (1, 2, rows, HEAD_DIM)]
    kv_keep, kv_send, q_keep, q_send = run_kernel(
        project_kernel, where, [mine, got, swapped, qkv_weight, l1, l2, l3, *far, r3, r2, r1],
        [S(shape, kind) for shape in shapes for kind in (F32, BF16)], [], 16,
        6 * rows * width * block, 6 * block * block * 8 + 4 * rows * width)
    kv = (kv_keep + shift(kv_send, "xl", 1)[:, ::-1].astype(F32)).astype(BF16)
    q_got = shift(q_send, "xl", 1)

    kv_r1, kv_l1 = both_ways(kv, kv)
    kv_r1, kv_l1, late_r1, late_l1 = step((kv_r1, kv_l1, late_r1, late_l1))
    kv_r2, kv_l2 = both_ways(kv_r1, kv_l1)
    kv_r3, kv_l3 = both_ways(kv_r2, kv_l2)
    kv_r3, kv_l3, out_weight = step((kv_r3, kv_l3, out_weight))
    out_weight = [out_weight, shift(out_weight, "xl", 1)]
    far_k, far_v = both_ways(kv_r3[:1], kv_l3[1:])
    far_k, far_v, late_r1, late_l1, conv_weight = step((far_k, far_v, late_r1, late_l1, conv_weight))
    conv_weight = lax.all_gather(conv_weight, "z", axis=0)

    late_r2, late_l2 = both_ways(late_r1, late_l1)
    own, away = run_kernel(
        attend_kernel, where, [q_keep, q_got, kv, kv_l1, kv_l2, kv_l3, kv_r3, kv_r2, kv_r1, far_k, far_v],
        [S((rows, HEAD_DIM), BF16)] * 2, [pltpu.VMEM((128, 16 * rows), F32)], 16,
        8 * rows * 16 * rows * HEAD_DIM, 4 << 20, 2 * rows * 16 * rows)
    back, late_r2, late_l2 = step((shift(away, "xl", 1), late_r2, late_l2))

    late_r3, late_l3 = both_ways(late_r2, late_l2)
    blocks_out = [S((blocks, rows, block), BF16)] * 2
    mine, other = run_kernel(
        project_out_kernel, where, [own, back] + out_weight, blocks_out, [], 12,
        2 * rows * block * width, 4 << 20)
    share = reduce_features(pair_sum(mine, other))
    frame_cols = lax.dynamic_slice_in_dim(frames, lax.axis_index(WT) * block, block, 1)
    mixed = (frame_cols.astype(F32) + share).astype(BF16)
    ready, late_r3, late_l3 = step((mixed, late_r3, late_l3))

    late_far = both_ways(late_r3[:2], late_l3[2:])
    mine, *late_far = step((gather_features(ready), *late_far))
    other = shift(mine, "c", 1)
    late = [late, late_l1, late_l2, late_l3, *late_far, late_r3, late_r2, late_r1]
    gated = run_kernel(
        glu_kernel, where, [mine, other, conv_norm_gain.reshape(1, width)] + late,
        S((rows, block), BF16), [pltpu.VMEM((2 * blocks, rows, block), BF16)], 16,
        4 * rows * block * width, 6 << 20)
    rim = 16
    before = shift(gated[rows - rim :], SEQ, 1)
    after = shift(gated[:rim], SEQ, -1)
    mine, other = run_kernel(
        conv_kernel, where,
        [gated, before, after, depth_kernel, norm_scale.reshape(1, block), norm_shift.reshape(1, block), conv_weight],
        blocks_out, [pltpu.VMEM((rows + 2 * rim, block), F32), pltpu.VMEM((rows, block), BF16)], 12,
        2 * rows * block * width, 4 << 20)
    return (mixed.astype(F32) + reduce_features(pair_sum(mine, other))).astype(BF16)


def solution(mesh):
    split = Mesh(mesh.devices.reshape(8, 2, 2, 4, 2), ("z", "xl", "xh", "y", "c"))
    in_specs = (
        P(SEQ, None),
        P(),
        P(None, SEQ, WT),
        P(SEQ, WT),
        P(),
        P(None, SEQ, WT),
        P(None, WT),
        P(WT),
        P(WT),
        P(SEQ, WT),
    )
    return jax.shard_map(local, mesh=split, in_specs=in_specs, out_specs=P(SEQ, WT), check_vma=False)
```

```python
import jax
import jax.numpy as jnp
from jax import lax
from jax.experimental import pallas as pl
from jax.experimental.pallas import tpu as pltpu
from jax.sharding import Mesh, PartitionSpec as P

HEAD_DIM = 128
BF16 = jnp.bfloat16
F32 = jnp.float32
SEQ = ("z", "xl")
WT = ("xh", "y", "c")
CHIPS = ("xh", "y")


def shift(value, axis, step):
    count = lax.axis_size(axis)
    return lax.ppermute(value, axis, [(i, (i + step) % count) for i in range(count)])


def smem():
    return pl.BlockSpec(memory_space=pltpu.SMEM)


def vmem():
    return pl.BlockSpec(memory_space=pltpu.VMEM)


def run_kernel(body, where, arrays, outs, scratch, megabytes, flops, moved, exps=0):
    return pl.pallas_call(
        body,
        out_shape=outs,
        in_specs=[smem()] + [vmem()] * len(arrays),
        out_specs=jax.tree.map(lambda _: vmem(), outs),
        scratch_shapes=scratch,
        compiler_params=pltpu.CompilerParams(vmem_limit_bytes=megabytes << 20),
        cost_estimate=pl.CostEstimate(flops=flops, bytes_accessed=moved, transcendentals=exps),
    )(where, *arrays)


def dot(a, b):
    return jnp.dot(a, b, preferred_element_type=F32)


def dot_t(a, b):
    return lax.dot_general(a, b, (((1,), (1,)), ((), ())), preferred_element_type=F32)


def norm_blocks_kernel(where, frames, gain, mine, other):
    rows, width = frames.shape
    blocks = mine.shape[0]
    block = mine.shape[2]
    z, xl, core = where[0], where[1], where[2]
    step_rows = 32

    def chunk(i, carry):
        r = pl.ds(pl.multiple_of(i * step_rows, step_rows), step_rows)
        wide = frames[r, :].astype(F32)
        mean = jnp.mean(wide, axis=-1, keepdims=True)
        centered = wide - mean
        scale = lax.rsqrt(jnp.mean(centered * centered, axis=-1, keepdims=True) + 1e-05)
        for out, first, parity in ((mine, 0, xl), (other, core * other.shape[0], 1 - xl)):
            for j in range(out.shape[0]):
                owner = lax.rem(z + first + j, blocks) * 2 + parity
                cols = pl.ds(pl.multiple_of(owner * block, block), block)
                part = (frames[r, cols].astype(F32) - mean) * scale * gain[:, cols]
                out[j, r, :] = part.astype(BF16)
        return carry

    lax.fori_loop(0, rows // step_rows, chunk, 0)


def project_kernel(where, mine, got, swapped, *refs):
    pieces, (kv_keep, kv_send, q_keep, q_send) = refs[:-4], refs[-4:]
    xl, core = where[1], where[2]
    low = [jnp.where(core == 0, got[j], swapped[j]) for j in range(4)]
    high = [jnp.where(core == 0, swapped[j], got[j]) for j in range(4)]
    half = pieces[4].shape[1]
    for m, keep, send, at in ((0, q_keep, q_send, 0), (1, kv_keep, kv_send, 0), (2, kv_keep, kv_send, 1)):
        for r, a in enumerate((mine, low + high)):
            acc = None
            for j in range(8):
                if j == 4:
                    term = dot(a[j][:, :half], pieces[4][m]) + dot(a[j][:, half:], pieces[5][m])
                else:
                    term = dot(a[j], pieces[j if j < 4 else j + 1][m])
                acc = term if acc is None else acc + term
            even, odd = acc[:, :HEAD_DIM], acc[:, HEAD_DIM:]
            keep[at, r] = jnp.where(xl == 0, even, odd)
            send[at, r] = jnp.where(xl == 0, odd, even).astype(BF16)


def attend_kernel(where, q_keep, q_got, *refs):
    parts, (mine, send), scores = refs[:-3], refs[-3:-1], refs[-1]
    scale = HEAD_DIM ** (-0.5)
    step_rows = 128
    chunk = parts[0].shape[1] * parts[0].shape[2]
    count = len(parts) - 1

    def piece(j, side):
        whole = parts[j][side] if j < count - 1 else parts[j + side][0]
        return whole.reshape(chunk, HEAD_DIM)

    for r, out in enumerate((mine, send)):
        for i in range(0, q_keep.shape[2], step_rows):
            query = (q_keep[0, r, i : i + step_rows] + q_got[0, 1 - r, i : i + step_rows].astype(F32)).astype(BF16)
            best = None
            for j in range(count):
                part = dot_t(query, piece(j, 0))
                scores[:, j * chunk : (j + 1) * chunk] = part
                top = jnp.max(part, axis=-1, keepdims=True)
                best = top if best is None else jnp.maximum(best, top)
            total = jnp.zeros((step_rows, 1), F32)
            acc = jnp.zeros((step_rows, HEAD_DIM), F32)
            for j in range(count):
                weights = jnp.exp((scores[:, j * chunk : (j + 1) * chunk] - best) * scale)
                total = total + jnp.sum(weights, axis=-1, keepdims=True)
                acc = acc + dot(weights.astype(BF16), piece(j, 1))
            out[i : i + step_rows, :] = (acc / total).astype(BF16)


def spread_out(inputs, pairs, places, mine, other, same):
    for (near, far), place in zip(pairs, places):
        a = dot_t(inputs, near).astype(BF16)
        b = dot_t(inputs, far).astype(BF16)
        mine[place] = jnp.where(same, a, b)
        other[place] = jnp.where(same, b, a)


def project_out_kernel(where, own, got, weight, far_weight, mine, other):
    xl = where[1]
    a, b = own[...], got[...]
    heads = jnp.concatenate([jnp.where(xl == 0, a, b), jnp.where(xl == 0, b, a)], axis=1)
    blocks, rows, block = mine.shape
    pairs = [(weight[j * block : (j + 1) * block], far_weight[j * block : (j + 1) * block]) for j in range(blocks)]
    spread_out(heads, pairs, range(blocks), mine, other, where[2] == xl)


def glu_kernel(where, mine, other, gain, *refs):
    pieces, (gated, normed) = refs[:-2], refs[-2:]
    blocks, rows, block = mine.shape
    z, xl = where[0], where[1]
    same = where[2] == xl
    step_rows = 32
    width = 2 * blocks * block

    def chunk(i, carry):
        r = pl.ds(pl.multiple_of(i * step_rows, step_rows), step_rows)
        parts = []
        for j in range(blocks):
            at = lax.rem(z + j, blocks)
            a, b = mine[at, r, :], other[at, r, :]
            parts += [jnp.where(same, a, b).astype(F32), jnp.where(same, b, a).astype(F32)]
        mean = jnp.sum(sum(parts), axis=-1, keepdims=True) / width
        square = sum((p - mean) * (p - mean) for p in parts)
        scale = lax.rsqrt(jnp.sum(square, axis=-1, keepdims=True) / width + 1e-05)
        for n, p in enumerate(parts):
            parity = xl if n % 2 == 0 else 1 - xl
            cols = pl.ds(pl.multiple_of((lax.rem(z + n // 2, blocks) * 2 + parity) * block, block), block)
            normed[n, r, :] = ((p - mean) * scale * gain[:, cols]).astype(BF16)
        return carry

    lax.fori_loop(0, rows // step_rows, chunk, 0)
    sums = [None, None]
    for n in range(2 * blocks):
        j = n // 2
        for m in range(2):
            if j == 4:
                weight = pieces[4 + m][n % 2]
            else:
                weight = pieces[j if j < 4 else j + 1][2 * m + n % 2]
            term = dot(normed[n], weight)
            sums[m] = term if sums[m] is None else sums[m] + term
    gated[...] = (sums[0] * jax.nn.sigmoid(sums[1])).astype(BF16)


def conv_kernel(where, gated, before, after, taps, scale, offset, *refs):
    pieces, (mine, other, padded, activated) = refs[:-4], refs[-4:]
    rows = gated.shape[0]
    rim = before.shape[0]
    seq = where[0] * 2 + where[1]
    padded[:rim] = jnp.where(seq > 0, before[...].astype(F32), 0.0)
    padded[rim : rim + rows] = gated[...].astype(F32)
    padded[rim + rows :] = jnp.where(seq < where[3] - 1, after[...].astype(F32), 0.0)
    count = taps.shape[0]
    first = rim - (count - 1) // 2
    for i in range(0, rows, 32):
        acc = None
        for k in range(count):
            term = taps[k : k + 1, :] * padded[i + first + k : i + first + k + 32, :]
            acc = term if acc is None else acc + term
        v = acc * scale[...] + offset[...]
        activated[i : i + 32, :] = (v * jax.nn.sigmoid(v)).astype(BF16)
    pairs = [(pieces[4][0], pieces[5][0]) if j == 4 else (pieces[j if j < 4 else j + 1][4], pieces[j if j < 4 else j + 1][5]) for j in range(8)]
    places = [lax.rem(where[0] + j, 8) for j in range(8)]
    spread_out(activated[...], pairs, places, mine, other, where[2] == where[1])


def both_ways(right, left):
    return shift(right, "z", 1), shift(left, "z", -1)


def pair_sum(mine, other):
    got = shift(other, "c", 1)
    return (mine.astype(F32) + got.astype(F32)).astype(BF16)


def reduce_features(pair):
    parts = lax.all_to_all(pair, CHIPS, 0, 0, tiled=True)
    return jnp.sum(parts.astype(F32), axis=0)


def gather_features(value):
    return lax.all_to_all(jnp.broadcast_to(value, (8,) + value.shape), CHIPS, 0, 0, tiled=True)


def local(
    frames,
    attn_norm_gain,
    qkv_weight,
    attn_out_weight,
    conv_norm_gain,
    glu_weight,
    depth_kernel,
    norm_scale,
    norm_shift,
    conv_out_weight,
):
    rows, width = frames.shape
    block = qkv_weight.shape[2]
    blocks = width // block // 2
    z, xl, core = (lax.axis_index(a) for a in ("z", "xl", "c"))
    where = jnp.stack([z, xl, core, lax.axis_size(SEQ)]).astype(jnp.int32)
    S = jax.ShapeDtypeStruct

    step = lax.optimization_barrier
    out_weight = lax.all_gather(attn_out_weight, "z", axis=0, tiled=True)
    late = jnp.concatenate([glu_weight, conv_out_weight[None]])
    late_far = shift(late, "xl", 1)

    half = block // 2
    r1, l1 = both_ways(qkv_weight, qkv_weight)
    mine, other = run_kernel(
        norm_blocks_kernel, where, [frames, attn_norm_gain.reshape(1, width)],
        [S((blocks, rows, block), BF16), S((blocks // 2, rows, block), BF16)], [], 16, 10 * rows * width, 4 * rows * width)
    got = shift(other, "xl", 1)
    r2, l2 = both_ways(r1, l1)
    r3, l3 = both_ways(r2, l2)
    far = both_ways(r3[:, :half], l3[:, half:])
    swapped, late_far = step((shift(got, "c", 1), late_far))
    late = jnp.stack([late, late_far], axis=1).reshape(6, block, block)
    shapes = [(2, 2, rows, HEAD_DIM), (1, 2, rows, HEAD_DIM)]
    kv_keep, kv_send, q_keep, q_send = run_kernel(
        project_kernel, where, [mine, got, swapped, qkv_weight, l1, l2, l3, *far, r3, r2, r1],
        [S(shape, kind) for shape in shapes for kind in (F32, BF16)], [], 24,
        6 * rows * width * block, 6 * block * block * 8 + 4 * rows * width)
    kv = (kv_keep + shift(kv_send, "xl", 1)[:, ::-1].astype(F32)).astype(BF16)
    q_got = shift(q_send, "xl", 1)

    kv_r1, kv_l1 = both_ways(kv, kv)
    kv_r2, kv_l2 = both_ways(kv_r1, kv_l1)
    kv_r2, kv_l2, q_got = step((kv_r2, kv_l2, q_got))
    kv_r3, kv_l3 = both_ways(kv_r2, kv_l2)
    out_weight = [out_weight, shift(out_weight, "xl", 1)]
    far_k, far_v = both_ways(kv_r3[:1], kv_l3[1:])
    far_k, far_v, late = step((far_k, far_v, late))

    late_r1, late_l1 = both_ways(late, late)
    own, away = run_kernel(
        attend_kernel, where, [q_keep, q_got, kv, kv_l1, kv_l2, kv_l3, kv_r3, kv_r2, kv_r1, far_k, far_v],
        [S((rows, HEAD_DIM), BF16)] * 2, [pltpu.VMEM((128, 16 * rows), F32)], 32,
        8 * rows * 16 * rows * HEAD_DIM, 4 << 20, 2 * rows * 16 * rows)
    back, late_r1, late_l1 = step((shift(away, "xl", 1), late_r1, late_l1))

    late_r2, late_l2 = both_ways(late_r1, late_l1)
    late_r3, late_l3 = both_ways(late_r2, late_l2)
    blocks_out = [S((blocks, rows, block), BF16)] * 2
    mine, other = run_kernel(
        project_out_kernel, where, [own, back] + out_weight, blocks_out, [], 16,
        2 * rows * block * width, 4 << 20)
    share = reduce_features(pair_sum(mine, other))
    frame_cols = lax.dynamic_slice_in_dim(frames, lax.axis_index(WT) * block, block, 1)
    mixed = (frame_cols.astype(F32) + share).astype(BF16)
    late_far = both_ways(late_r3[:2], late_l3[2:4])
    late_last = both_ways(late_r3[4:5], late_l3[5:])
    mine, *late_far = step((gather_features(mixed), *late_far))
    other = shift(mine, "c", 1)
    ahead, behind = [late, late_l1, late_l2, late_l3], [late_r3, late_r2, late_r1]
    gated = run_kernel(
        glu_kernel, where, [mine, other, conv_norm_gain.reshape(1, width), *ahead, *late_far, *behind],
        S((rows, block), BF16), [pltpu.VMEM((2 * blocks, rows, block), BF16)], 24,
        4 * rows * block * width, 6 << 20)
    rim = 16
    before = shift(gated[rows - rim :], SEQ, 1)
    after = shift(gated[:rim], SEQ, -1)
    mine, other = run_kernel(
        conv_kernel, where,
        [gated, before, after, depth_kernel, norm_scale.reshape(1, block), norm_shift.reshape(1, block), *ahead, *late_last, *behind],
        blocks_out, [pltpu.VMEM((rows + 2 * rim, block), F32), pltpu.VMEM((rows, block), BF16)], 16,
        2 * rows * block * width, 4 << 20)
    return (mixed.astype(F32) + reduce_features(pair_sum(mine, other))).astype(BF16)


def solution(mesh):
    split = Mesh(mesh.devices.reshape(8, 2, 2, 4, 2), ("z", "xl", "xh", "y", "c"))
    in_specs = (
        P(SEQ, None),
        P(),
        P(None, SEQ, WT),
        P(SEQ, WT),
        P(),
        P(None, SEQ, WT),
        P(None, WT),
        P(WT),
        P(WT),
        P(SEQ, WT),
    )
    return jax.shard_map(local, mesh=split, in_specs=in_specs, out_specs=P(SEQ, WT), check_vma=False)
```

```python
import jax
import jax.numpy as jnp
from jax import lax
from jax.experimental import pallas as pl
from jax.experimental.pallas import tpu as pltpu
from jax.sharding import Mesh, PartitionSpec as P

HEAD_DIM = 128
BF16 = jnp.bfloat16
F32 = jnp.float32
SEQ = ("z", "xl")
WT = ("xh", "y", "c")
CHIPS = ("xh", "y")


def shift(value, axis, step):
    count = lax.axis_size(axis)
    return lax.ppermute(value, axis, [(i, (i + step) % count) for i in range(count)])


def smem():
    return pl.BlockSpec(memory_space=pltpu.SMEM)


def vmem():
    return pl.BlockSpec(memory_space=pltpu.VMEM)


def hbm():
    return pl.BlockSpec(memory_space=pltpu.HBM)


def run_kernel(body, where, arrays, outs, scratch, megabytes, flops, moved, exps=0, pinned=()):
    return pl.pallas_call(
        body,
        out_shape=outs,
        in_specs=[smem()] + [vmem()] * len(arrays) + [hbm()] * len(pinned),
        out_specs=jax.tree.map(lambda _: vmem(), outs),
        scratch_shapes=scratch,
        compiler_params=pltpu.CompilerParams(vmem_limit_bytes=megabytes << 20),
        cost_estimate=pl.CostEstimate(flops=flops, bytes_accessed=moved, transcendentals=exps),
    )(where, *arrays, *pinned)


def fetch(sources, places, sems):
    copies = [pltpu.make_async_copy(a, b, sems.at[n]) for n, (a, b) in enumerate(zip(sources, places))]
    for copy in copies:
        copy.start()
    return copies


def ring_places(buffer, first, second):
    return [buffer.at[j] for j in range(4)] + [first, second] + [buffer.at[j] for j in range(5, 8)]


def dot(a, b):
    return jnp.dot(a, b, preferred_element_type=F32)


def dot_t(a, b):
    return lax.dot_general(a, b, (((1,), (1,)), ((), ())), preferred_element_type=F32)


def norm_blocks_kernel(where, frames, gain, mine, other):
    rows, width = frames.shape
    blocks = mine.shape[0]
    block = mine.shape[2]
    z, xl, core = where[0], where[1], where[2]
    step_rows = 32

    def chunk(i, carry):
        r = pl.ds(pl.multiple_of(i * step_rows, step_rows), step_rows)
        wide = frames[r, :].astype(F32)
        mean = jnp.mean(wide, axis=-1, keepdims=True)
        centered = wide - mean
        scale = lax.rsqrt(jnp.mean(centered * centered, axis=-1, keepdims=True) + 1e-05)
        for out, first, parity in ((mine, 0, xl), (other, core * other.shape[0], 1 - xl)):
            for j in range(out.shape[0]):
                owner = lax.rem(z + first + j, blocks) * 2 + parity
                cols = pl.ds(pl.multiple_of(owner * block, block), block)
                part = (frames[r, cols].astype(F32) - mean) * scale * gain[:, cols]
                out[j, r, :] = part.astype(BF16)
        return carry

    lax.fori_loop(0, rows // step_rows, chunk, 0)


def project_kernel(where, mine, got, swapped, *refs):
    pieces, (kv_keep, kv_send, q_keep, q_send, weights, sems) = refs[:-6], refs[-6:]
    xl, core = where[1], where[2]
    low = [jnp.where(core == 0, got[j], swapped[j]) for j in range(4)]
    high = [jnp.where(core == 0, swapped[j], got[j]) for j in range(4)]
    half = pieces[4].shape[1]
    copies = fetch(pieces, ring_places(weights, weights.at[4, :, :half], weights.at[4, :, half:]), sems)
    for copy in copies:
        copy.wait()
    for m, keep, send, at in ((0, q_keep, q_send, 0), (1, kv_keep, kv_send, 0), (2, kv_keep, kv_send, 1)):
        for r, a in enumerate((mine, low + high)):
            acc = None
            for j in range(8):
                term = dot(a[j], weights[j, m])
                acc = term if acc is None else acc + term
            even, odd = acc[:, :HEAD_DIM], acc[:, HEAD_DIM:]
            keep[at, r] = jnp.where(xl == 0, even, odd)
            send[at, r] = jnp.where(xl == 0, odd, even).astype(BF16)


def attend_kernel(where, q_keep, q_got, *refs):
    parts, (mine, send, scores, held, sems) = refs[:-5], refs[-5:]
    scale = HEAD_DIM ** (-0.5)
    step_rows = 128
    chunk = held.shape[2] * held.shape[3]
    count = len(parts)
    copies = fetch(parts, [held.at[j] for j in range(count)], sems)
    for copy in copies:
        copy.wait()

    def piece(j, side):
        return held[j, side].reshape(chunk, HEAD_DIM)

    for r, out in enumerate((mine, send)):
        for i in range(0, q_keep.shape[2], step_rows):
            query = (q_keep[0, r, i : i + step_rows] + q_got[0, 1 - r, i : i + step_rows].astype(F32)).astype(BF16)
            best = None
            for j in range(count):
                part = dot_t(query, piece(j, 0))
                scores[:, j * chunk : (j + 1) * chunk] = part
                top = jnp.max(part, axis=-1, keepdims=True)
                best = top if best is None else jnp.maximum(best, top)
            total = jnp.zeros((step_rows, 1), F32)
            acc = jnp.zeros((step_rows, HEAD_DIM), F32)
            for j in range(count):
                weights = jnp.exp((scores[:, j * chunk : (j + 1) * chunk] - best) * scale)
                total = total + jnp.sum(weights, axis=-1, keepdims=True)
                acc = acc + dot(weights.astype(BF16), piece(j, 1))
            out[i : i + step_rows, :] = (acc / total).astype(BF16)


def spread_out(inputs, pairs, places, mine, other, same):
    for (near, far), place in zip(pairs, places):
        a = dot_t(inputs, near).astype(BF16)
        b = dot_t(inputs, far).astype(BF16)
        mine[place] = jnp.where(same, a, b)
        other[place] = jnp.where(same, b, a)


def project_out_kernel(where, own, got, weight, far_weight, mine, other):
    xl = where[1]
    a, b = own[...], got[...]
    heads = jnp.concatenate([jnp.where(xl == 0, a, b), jnp.where(xl == 0, b, a)], axis=1)
    blocks, rows, block = mine.shape
    pairs = [(weight[j * block : (j + 1) * block], far_weight[j * block : (j + 1) * block]) for j in range(blocks)]
    spread_out(heads, pairs, range(blocks), mine, other, where[2] == xl)


def glu_kernel(where, mine, other, gain, *refs):
    pieces, (gated, normed, weights, sems) = refs[:-4], refs[-4:]
    blocks, rows, block = mine.shape
    sources = [piece.at[:4] if n not in (4, 5) else piece for n, piece in enumerate(pieces)]
    copies = fetch(sources, ring_places(weights, weights.at[4, :2], weights.at[4, 2:]), sems)
    z, xl = where[0], where[1]
    same = where[2] == xl
    step_rows = 32
    width = 2 * blocks * block

    def chunk(i, carry):
        r = pl.ds(pl.multiple_of(i * step_rows, step_rows), step_rows)
        parts = []
        for j in range(blocks):
            at = lax.rem(z + j, blocks)
            a, b = mine[at, r, :], other[at, r, :]
            parts += [jnp.where(same, a, b).astype(F32), jnp.where(same, b, a).astype(F32)]
        mean = jnp.sum(sum(parts), axis=-1, keepdims=True) / width
        square = sum((p - mean) * (p - mean) for p in parts)
        scale = lax.rsqrt(jnp.sum(square, axis=-1, keepdims=True) / width + 1e-05)
        for n, p in enumerate(parts):
            parity = xl if n % 2 == 0 else 1 - xl
            cols = pl.ds(pl.multiple_of((lax.rem(z + n // 2, blocks) * 2 + parity) * block, block), block)
            normed[n, r, :] = ((p - mean) * scale * gain[:, cols]).astype(BF16)
        return carry

    lax.fori_loop(0, rows // step_rows, chunk, 0)
    for copy in copies:
        copy.wait()
    sums = [None, None]
    for n in range(2 * blocks):
        j = n // 2
        for m in range(2):
            term = dot(normed[n], weights[j, 2 * m + n % 2])
            sums[m] = term if sums[m] is None else sums[m] + term
    gated[...] = (sums[0] * jax.nn.sigmoid(sums[1])).astype(BF16)


def conv_kernel(where, gated, before, after, taps, scale, offset, *refs):
    pieces, (mine, other, padded, activated, weights, sems) = refs[:-6], refs[-6:]
    sources = [piece.at[4:] if n not in (4, 5) else piece for n, piece in enumerate(pieces)]
    copies = fetch(sources, ring_places(weights, weights.at[4, :1], weights.at[4, 1:]), sems)
    rows = gated.shape[0]
    rim = before.shape[0]
    seq = where[0] * 2 + where[1]
    padded[:rim] = jnp.where(seq > 0, before[...].astype(F32), 0.0)
    padded[rim : rim + rows] = gated[...].astype(F32)
    padded[rim + rows :] = jnp.where(seq < where[3] - 1, after[...].astype(F32), 0.0)
    count = taps.shape[0]
    first = rim - (count - 1) // 2
    for i in range(0, rows, 32):
        acc = None
        for k in range(count):
            term = taps[k : k + 1, :] * padded[i + first + k : i + first + k + 32, :]
            acc = term if acc is None else acc + term
        v = acc * scale[...] + offset[...]
        activated[i : i + 32, :] = (v * jax.nn.sigmoid(v)).astype(BF16)
    for copy in copies:
        copy.wait()
    pairs = [(weights[j, 0], weights[j, 1]) for j in range(8)]
    places = [lax.rem(where[0] + j, 8) for j in range(8)]
    spread_out(activated[...], pairs, places, mine, other, where[2] == where[1])


def residual_kernel(where, parts, frames, mixed, copies, held, sem):
    block = mixed.shape[1]
    cols = pl.ds(pl.multiple_of(where[4] * block, block), block)
    copy = pltpu.make_async_copy(frames.at[:, cols], held, sem)
    copy.start()
    total = parts[0].astype(F32)
    for j in range(1, parts.shape[0]):
        total = total + parts[j].astype(F32)
    copy.wait()
    result = (held[...].astype(F32) + total).astype(BF16)
    mixed[...] = result
    for j in range(copies.shape[0]):
        copies[j] = result


def both_ways(right, left):
    return shift(right, "z", 1), shift(left, "z", -1)


def pair_sum(mine, other):
    got = shift(other, "c", 1)
    return (mine.astype(F32) + got.astype(F32)).astype(BF16)


def exchange(parts):
    return lax.all_to_all(parts, CHIPS, 0, 0, tiled=True)


def local(
    frames,
    attn_norm_gain,
    qkv_weight,
    attn_out_weight,
    conv_norm_gain,
    glu_weight,
    depth_kernel,
    norm_scale,
    norm_shift,
    conv_out_weight,
):
    rows, width = frames.shape
    block = qkv_weight.shape[2]
    blocks = width // block // 2
    z, xl, core = (lax.axis_index(a) for a in ("z", "xl", "c"))
    where = jnp.stack([z, xl, core, lax.axis_size(SEQ), lax.axis_index(WT)]).astype(jnp.int32)
    S = jax.ShapeDtypeStruct

    step = lax.optimization_barrier
    out_weight = lax.all_gather(attn_out_weight, "z", axis=0, tiled=True)
    late = jnp.concatenate([glu_weight, conv_out_weight[None]])
    late_far = shift(late, "xl", 1)

    half = block // 2
    r1, l1 = both_ways(qkv_weight, qkv_weight)
    mine, other = run_kernel(
        norm_blocks_kernel, where, [frames, attn_norm_gain.reshape(1, width)],
        [S((blocks, rows, block), BF16), S((blocks // 2, rows, block), BF16)], [], 16, 10 * rows * width, 4 * rows * width)
    got = shift(other, "xl", 1)
    r2, l2 = both_ways(r1, l1)
    r3, l3 = both_ways(r2, l2)
    far = both_ways(r3[:, :half], l3[:, half:])
    swapped, late_far = step((shift(got, "c", 1), late_far))
    late = jnp.stack([late, late_far], axis=1).reshape(6, block, block)
    shapes = [(2, 2, rows, HEAD_DIM), (1, 2, rows, HEAD_DIM)]
    kv_keep, kv_send, q_keep, q_send = run_kernel(
        project_kernel, where, [mine, got, swapped],
        [S(shape, kind) for shape in shapes for kind in (F32, BF16)],
        [pltpu.VMEM((blocks, 3, block, block), BF16), pltpu.SemaphoreType.DMA((9,))], 60,
        6 * rows * width * block, 6 * block * block * 8 + 4 * rows * width,
        pinned=[qkv_weight, l1, l2, l3, *far, r3, r2, r1])
    kv = (kv_keep + shift(kv_send, "xl", 1)[:, ::-1].astype(F32)).astype(BF16)
    q_got = shift(q_send, "xl", 1)

    kv_r1, kv_l1 = both_ways(kv, kv)
    kv_r2, kv_l2 = both_ways(kv_r1, kv_l1)
    kv_r2, kv_l2, q_got = step((kv_r2, kv_l2, q_got))
    kv_r3, kv_l3 = both_ways(kv_r2, kv_l2)
    out_weight = [out_weight, shift(out_weight, "xl", 1)]
    kv_r3, kv_l3 = step((kv_r3, kv_l3))
    kv_r4, late = step((shift(kv_r3, "z", 1), late))

    late_r1, late_l1 = both_ways(late, late)
    own, away = run_kernel(
        attend_kernel, where, [q_keep, q_got], [S((rows, HEAD_DIM), BF16)] * 2,
        [pltpu.VMEM((128, 16 * rows), F32), pltpu.VMEM((blocks, 2, 2, rows, HEAD_DIM), BF16), pltpu.SemaphoreType.DMA((blocks,))], 32,
        8 * rows * 16 * rows * HEAD_DIM, 4 << 20, 2 * rows * 16 * rows,
        pinned=[kv, kv_l1, kv_l2, kv_l3, kv_r4, kv_r3, kv_r2, kv_r1])
    back, late_r1, late_l1 = step((shift(away, "xl", 1), late_r1, late_l1))

    late_r2, late_l2 = both_ways(late_r1, late_l1)
    late_r3, late_l3 = both_ways(late_r2, late_l2)
    blocks_out = [S((blocks, rows, block), BF16)] * 2
    mine, other = run_kernel(
        project_out_kernel, where, [own, back] + out_weight, blocks_out, [], 16,
        2 * rows * block * width, 4 << 20)
    mixed, copies = run_kernel(
        residual_kernel, where, [exchange(pair_sum(mine, other))],
        [S((rows, block), BF16), S((blocks, rows, block), BF16)],
        [pltpu.VMEM((rows, block), BF16), pltpu.SemaphoreType.DMA], 16, 10 * rows * block, 20 * rows * block, pinned=[frames])
    late_far = both_ways(late_r3[:2], late_l3[2:4])
    late_last = both_ways(late_r3[4:5], late_l3[5:])
    mine, *late_far = step((exchange(copies), *late_far))
    other = shift(mine, "c", 1)
    ahead, behind = [late, late_l1, late_l2, late_l3], [late_r3, late_r2, late_r1]
    gated = run_kernel(
        glu_kernel, where, [mine, other, conv_norm_gain.reshape(1, width)],
        S((rows, block), BF16),
        [pltpu.VMEM((2 * blocks, rows, block), BF16), pltpu.VMEM((blocks, 4, block, block), BF16), pltpu.SemaphoreType.DMA((9,))], 24,
        4 * rows * block * width, 6 << 20, pinned=[*ahead, *late_far, *behind])
    rim = 16
    before = shift(gated[rows - rim :], SEQ, 1)
    after = shift(gated[:rim], SEQ, -1)
    mine, other = run_kernel(
        conv_kernel, where,
        [gated, before, after, depth_kernel, norm_scale.reshape(1, block), norm_shift.reshape(1, block)],
        blocks_out,
        [pltpu.VMEM((rows + 2 * rim, block), F32), pltpu.VMEM((rows, block), BF16),
         pltpu.VMEM((blocks, 2, block, block), BF16), pltpu.SemaphoreType.DMA((9,))], 16,
        2 * rows * block * width, 4 << 20, pinned=[*ahead, *late_last, *behind])
    total = jnp.sum(exchange(pair_sum(mine, other)).astype(F32), axis=0)
    return (mixed.astype(F32) + total).astype(BF16)


def solution(mesh):
    split = Mesh(mesh.devices.reshape(8, 2, 2, 4, 2), ("z", "xl", "xh", "y", "c"))
    in_specs = (
        P(SEQ, None),
        P(),
        P(None, SEQ, WT),
        P(SEQ, WT),
        P(),
        P(None, SEQ, WT),
        P(None, WT),
        P(WT),
        P(WT),
        P(SEQ, WT),
    )
    return jax.shard_map(local, mesh=split, in_specs=in_specs, out_specs=P(SEQ, WT), check_vma=False)
```

```python
import jax
import jax.numpy as jnp
from jax import lax
from jax.experimental import pallas as pl
from jax.experimental.pallas import tpu as pltpu
from jax.sharding import Mesh, PartitionSpec as P

HEAD_DIM = 128
BF16 = jnp.bfloat16
F32 = jnp.float32
SEQ = ("z", "xl")
WT = ("xh", "y", "c")
CHIPS = ("xh", "y")


def shift(value, axis, step):
    count = lax.axis_size(axis)
    return lax.ppermute(value, axis, [(i, (i + step) % count) for i in range(count)])


def smem():
    return pl.BlockSpec(memory_space=pltpu.SMEM)


def vmem():
    return pl.BlockSpec(memory_space=pltpu.VMEM)


def hbm():
    return pl.BlockSpec(memory_space=pltpu.HBM)


def run_kernel(body, where, arrays, outs, scratch, megabytes, flops, moved, exps=0, pinned=(), out_specs=None):
    return pl.pallas_call(
        body,
        out_shape=outs,
        in_specs=[smem()] + [vmem()] * len(arrays) + [hbm()] * len(pinned),
        out_specs=out_specs or jax.tree.map(lambda _: vmem(), outs),
        scratch_shapes=scratch,
        compiler_params=pltpu.CompilerParams(vmem_limit_bytes=megabytes << 20),
        cost_estimate=pl.CostEstimate(flops=flops, bytes_accessed=moved, transcendentals=exps),
    )(where, *arrays, *pinned)


def fetch(sources, places, sems):
    copies = [pltpu.make_async_copy(a, b, sems.at[n]) for n, (a, b) in enumerate(zip(sources, places))]
    for copy in copies:
        copy.start()
    return copies


def ring_places(buffer, first, second):
    return [buffer.at[j] for j in range(4)] + [first, second] + [buffer.at[j] for j in range(5, 8)]


def dot(a, b):
    return jnp.dot(a, b, preferred_element_type=F32)


def dot_t(a, b):
    return lax.dot_general(a, b, (((1,), (1,)), ((), ())), preferred_element_type=F32)


def norm_blocks_kernel(where, frames, gain, mine, other):
    rows, width = frames.shape
    blocks = mine.shape[0]
    block = mine.shape[2]
    z, xl, core = where[0], where[1], where[2]
    step_rows = 32

    def chunk(i, carry):
        r = pl.ds(pl.multiple_of(i * step_rows, step_rows), step_rows)
        wide = frames[r, :].astype(F32)
        mean = jnp.mean(wide, axis=-1, keepdims=True)
        centered = wide - mean
        scale = lax.rsqrt(jnp.mean(centered * centered, axis=-1, keepdims=True) + 1e-05)
        for out, first, parity in ((mine, 0, xl), (other, core * other.shape[0], 1 - xl)):
            for j in range(out.shape[0]):
                owner = lax.rem(z + first + j, blocks) * 2 + parity
                cols = pl.ds(pl.multiple_of(owner * block, block), block)
                part = (frames[r, cols].astype(F32) - mean) * scale * gain[:, cols]
                out[j, r, :] = part.astype(BF16)
        return carry

    lax.fori_loop(0, rows // step_rows, chunk, 0)


def project_kernel(where, mine, got, swapped, *refs):
    pieces, (kv_keep, kv_send, q_keep, q_send, weights, sems) = refs[:-6], refs[-6:]
    xl, core = where[1], where[2]
    low = [jnp.where(core == 0, got[j], swapped[j]) for j in range(4)]
    high = [jnp.where(core == 0, swapped[j], got[j]) for j in range(4)]
    half = pieces[4].shape[1]
    places = [weights.at[:, j] for j in range(4)] + [weights.at[:, 4, :half], weights.at[:, 4, half:]] + [weights.at[:, j] for j in range(5, 8)]
    copies = {}
    for m in (1, 2, 0):
        copies[m] = fetch([piece.at[m] for piece in pieces], [place.at[m] for place in places], sems.at[m])
    for m, keep, send, at in ((1, kv_keep, kv_send, 0), (2, kv_keep, kv_send, 1), (0, q_keep, q_send, 0)):
        for copy in copies[m]:
            copy.wait()
        for r, a in enumerate((mine, low + high)):
            acc = None
            for j in range(8):
                term = dot(a[j], weights[m, j])
                acc = term if acc is None else acc + term
            even, odd = acc[:, :HEAD_DIM], acc[:, HEAD_DIM:]
            keep[at, r] = jnp.where(xl == 0, even, odd)
            send[at, r] = jnp.where(xl == 0, odd, even).astype(BF16)


def attend_kernel(where, q_keep, q_got, *refs):
    parts, (mine, send, scores, held, sems) = refs[:-5], refs[-5:]
    scale = HEAD_DIM ** (-0.5)
    step_rows = 128
    chunk = held.shape[2] * held.shape[3]
    count = len(parts)
    copies = fetch(parts, [held.at[j] for j in range(count)], sems)
    for copy in copies:
        copy.wait()

    def piece(j, side):
        return held[j, side].reshape(chunk, HEAD_DIM)

    for r, out in enumerate((mine, send)):
        for i in range(0, q_keep.shape[2], step_rows):
            query = (q_keep[0, r, i : i + step_rows] + q_got[0, 1 - r, i : i + step_rows].astype(F32)).astype(BF16)
            best = None
            for j in range(count):
                part = dot_t(query, piece(j, 0))
                scores[:, j * chunk : (j + 1) * chunk] = part
                top = jnp.max(part, axis=-1, keepdims=True)
                best = top if best is None else jnp.maximum(best, top)
            total = jnp.zeros((step_rows, 1), F32)
            acc = jnp.zeros((step_rows, HEAD_DIM), F32)
            for j in range(count):
                weights = jnp.exp((scores[:, j * chunk : (j + 1) * chunk] - best) * scale)
                total = total + jnp.sum(weights, axis=-1, keepdims=True)
                acc = acc + dot(weights.astype(BF16), piece(j, 1))
            out[i : i + step_rows, :] = (acc / total).astype(BF16)


def spread_out(inputs, pairs, places, mine, other, same):
    for (near, far), place in zip(pairs, places):
        a = dot_t(inputs, near).astype(BF16)
        b = dot_t(inputs, far).astype(BF16)
        mine[place] = jnp.where(same, a, b)
        other[place] = jnp.where(same, b, a)


def project_out_kernel(where, own, got, weight, far_weight, mine, other):
    xl = where[1]
    a, b = own[...], got[...]
    heads = jnp.concatenate([jnp.where(xl == 0, a, b), jnp.where(xl == 0, b, a)], axis=1)
    blocks, rows, block = mine.shape
    pairs = [(weight[j * block : (j + 1) * block], far_weight[j * block : (j + 1) * block]) for j in range(blocks)]
    spread_out(heads, pairs, range(blocks), mine, other, where[2] == xl)


def glu_kernel(where, mine, other, gain, *refs):
    pieces, (gated, normed, weights, sems) = refs[:-4], refs[-4:]
    blocks, rows, block = mine.shape
    sources = [piece.at[:4] for piece in pieces]
    sources[4:6] = [pieces[4], pieces[5].at[:1]]
    copies = fetch(sources, ring_places(weights, weights.at[4, :3], weights.at[4, 3:]), sems)
    z, xl = where[0], where[1]
    same = where[2] == xl
    step_rows = 32
    width = 2 * blocks * block

    def chunk(i, carry):
        r = pl.ds(pl.multiple_of(i * step_rows, step_rows), step_rows)
        parts = []
        for j in range(blocks):
            at = lax.rem(z + j, blocks)
            a, b = mine[at, r, :], other[at, r, :]
            parts += [jnp.where(same, a, b).astype(F32), jnp.where(same, b, a).astype(F32)]
        mean = jnp.sum(sum(parts), axis=-1, keepdims=True) / width
        square = sum((p - mean) * (p - mean) for p in parts)
        scale = lax.rsqrt(jnp.sum(square, axis=-1, keepdims=True) / width + 1e-05)
        for n, p in enumerate(parts):
            parity = xl if n % 2 == 0 else 1 - xl
            cols = pl.ds(pl.multiple_of((lax.rem(z + n // 2, blocks) * 2 + parity) * block, block), block)
            normed[n, r, :] = ((p - mean) * scale * gain[:, cols]).astype(BF16)
        return carry

    lax.fori_loop(0, rows // step_rows, chunk, 0)
    for copy in copies:
        copy.wait()
    sums = [None, None]
    for n in range(2 * blocks):
        j = n // 2
        for m in range(2):
            term = dot(normed[n], weights[j, 2 * m + n % 2])
            sums[m] = term if sums[m] is None else sums[m] + term
    gated[...] = (sums[0] * jax.nn.sigmoid(sums[1])).astype(BF16)


def conv_kernel(where, gated, before, after, taps, scale, offset, *refs):
    pieces, (mine, other, padded, activated, weights, sems) = refs[:-6], refs[-6:]
    sources = [piece.at[4:] for n, piece in enumerate(pieces) if n not in (4, 5)]
    sources.append(pieces[5].at[1:])
    copies = fetch(sources, [weights.at[j] for j in (0, 1, 2, 3, 5, 6, 7, 4)], sems)
    rows = gated.shape[0]
    rim = before.shape[0]
    seq = where[0] * 2 + where[1]
    padded[:rim] = jnp.where(seq > 0, before[...].astype(F32), 0.0)
    padded[rim : rim + rows] = gated[...].astype(F32)
    padded[rim + rows :] = jnp.where(seq < where[3] - 1, after[...].astype(F32), 0.0)
    count = taps.shape[0]
    first = rim - (count - 1) // 2
    for i in range(0, rows, 32):
        acc = None
        for k in range(count):
            term = taps[k : k + 1, :] * padded[i + first + k : i + first + k + 32, :]
            acc = term if acc is None else acc + term
        v = acc * scale[...] + offset[...]
        activated[i : i + 32, :] = (v * jax.nn.sigmoid(v)).astype(BF16)
    for copy in copies:
        copy.wait()
    pairs = [(weights[j, 0], weights[j, 1]) for j in range(8)]
    places = [lax.rem(where[0] + j, 8) for j in range(8)]
    spread_out(activated[...], pairs, places, mine, other, where[2] == where[1])


def residual_kernel(where, parts, frames, mixed, copies, held, sem, sems):
    block = mixed.shape[1]
    cols = pl.ds(pl.multiple_of(where[4] * block, block), block)
    copy = pltpu.make_async_copy(frames.at[:, cols], held, sem)
    copy.start()
    total = parts[0].astype(F32)
    for j in range(1, parts.shape[0]):
        total = total + parts[j].astype(F32)
    copy.wait()
    result = (held[...].astype(F32) + total).astype(BF16)
    mixed[...] = result
    count = copies.shape[0]
    for out in fetch([mixed] * count, [copies.at[j] for j in range(count)], sems):
        out.wait()


def both_ways(right, left):
    return shift(right, "z", 1), shift(left, "z", -1)


def pair_sum(mine, other):
    got = shift(other, "c", 1)
    return (mine.astype(F32) + got.astype(F32)).astype(BF16)


def exchange(parts):
    return lax.all_to_all(parts, CHIPS, 0, 0, tiled=True)


def local(
    frames,
    attn_norm_gain,
    qkv_weight,
    attn_out_weight,
    conv_norm_gain,
    glu_weight,
    depth_kernel,
    norm_scale,
    norm_shift,
    conv_out_weight,
):
    rows, width = frames.shape
    block = qkv_weight.shape[2]
    blocks = width // block // 2
    z, xl, core = (lax.axis_index(a) for a in ("z", "xl", "c"))
    where = jnp.stack([z, xl, core, lax.axis_size(SEQ), lax.axis_index(WT)]).astype(jnp.int32)
    S = jax.ShapeDtypeStruct

    step = lax.optimization_barrier
    out_weight = lax.all_gather(attn_out_weight, "z", axis=0, tiled=True)
    late = jnp.concatenate([glu_weight, conv_out_weight[None]])
    late_far = shift(late, "xl", 1)

    half = block // 2
    r1, l1 = both_ways(qkv_weight, qkv_weight)
    mine, other = run_kernel(
        norm_blocks_kernel, where, [frames, attn_norm_gain.reshape(1, width)],
        [S((blocks, rows, block), BF16), S((blocks // 2, rows, block), BF16)], [], 16, 10 * rows * width, 4 * rows * width)
    got = shift(other, "xl", 1)
    r2, l2 = both_ways(r1, l1)
    r3, l3 = both_ways(r2, l2)
    far = both_ways(r3[:, :half], l3[:, half:])
    swapped, late_far = step((shift(got, "c", 1), late_far))
    late = jnp.stack([late, late_far], axis=1).reshape(6, block, block)
    shapes = [(2, 2, rows, HEAD_DIM), (1, 2, rows, HEAD_DIM)]
    kv_keep, kv_send, q_keep, q_send = run_kernel(
        project_kernel, where, [mine, got, swapped],
        [S(shape, kind) for shape in shapes for kind in (F32, BF16)],
        [pltpu.VMEM((3, blocks, block, block), BF16), pltpu.SemaphoreType.DMA((3, 9))], 60,
        6 * rows * width * block, 6 * block * block * 8 + 4 * rows * width,
        pinned=[qkv_weight, l1, l2, l3, *far, r3, r2, r1])
    kv = (kv_keep + shift(kv_send, "xl", 1)[:, ::-1].astype(F32)).astype(BF16)
    q_got = shift(q_send, "xl", 1)

    kv_r1, kv_l1 = both_ways(kv, kv)
    kv_r1, kv_l1, q_got = step((kv_r1, kv_l1, q_got))
    kv_r2, kv_l2 = both_ways(kv_r1, kv_l1)
    kv_r3, kv_l3 = both_ways(kv_r2, kv_l2)
    out_weight = [out_weight, shift(out_weight, "xl", 1)]
    kv_r3, kv_l3 = step((kv_r3, kv_l3))
    kv_r4, late = step((shift(kv_r3, "z", 1), late))

    late_r1, late_l1 = both_ways(late, late)
    own, away = run_kernel(
        attend_kernel, where, [q_keep, q_got], [S((rows, HEAD_DIM), BF16)] * 2,
        [pltpu.VMEM((128, 16 * rows), F32), pltpu.VMEM((blocks, 2, 2, rows, HEAD_DIM), BF16), pltpu.SemaphoreType.DMA((blocks,))], 32,
        8 * rows * 16 * rows * HEAD_DIM, 4 << 20, 2 * rows * 16 * rows,
        pinned=[kv, kv_l1, kv_l2, kv_l3, kv_r4, kv_r3, kv_r2, kv_r1])
    back = shift(away, "xl", 1)
    blocks_out = [S((blocks, rows, block), BF16)] * 2
    mine, other = run_kernel(
        project_out_kernel, where, [own, back] + out_weight, blocks_out, [], 16,
        2 * rows * block * width, 4 << 20)
    other, late_r1, late_l1 = step((other, late_r1, late_l1))
    late_r2, late_l2 = both_ways(late_r1, late_l1)
    late_r3, late_l3 = both_ways(late_r2, late_l2)
    mixed, copies = run_kernel(
        residual_kernel, where, [exchange(pair_sum(mine, other))],
        [S((rows, block), BF16), S((blocks, rows, block), BF16)],
        [pltpu.VMEM((rows, block), BF16), pltpu.SemaphoreType.DMA, pltpu.SemaphoreType.DMA((blocks,))], 16,
        10 * rows * block, 20 * rows * block, pinned=[frames], out_specs=[vmem(), hbm()])
    late_far = both_ways(late_r3[:3], late_l3[3:])
    mine, *late_far = step((exchange(copies), *late_far))
    other = shift(mine, "c", 1)
    ahead, behind = [late, late_l1, late_l2, late_l3], [late_r3, late_r2, late_r1]
    gated = run_kernel(
        glu_kernel, where, [mine, other, conv_norm_gain.reshape(1, width)],
        S((rows, block), BF16),
        [pltpu.VMEM((2 * blocks, rows, block), BF16), pltpu.VMEM((blocks, 4, block, block), BF16), pltpu.SemaphoreType.DMA((9,))], 24,
        4 * rows * block * width, 6 << 20, pinned=[*ahead, *late_far, *behind])
    rim = 16
    before = shift(gated[rows - rim :], SEQ, 1)
    after = shift(gated[:rim], SEQ, -1)
    mine, other = run_kernel(
        conv_kernel, where,
        [gated, before, after, depth_kernel, norm_scale.reshape(1, block), norm_shift.reshape(1, block)],
        blocks_out,
        [pltpu.VMEM((rows + 2 * rim, block), F32), pltpu.VMEM((rows, block), BF16),
         pltpu.VMEM((blocks, 2, block, block), BF16), pltpu.SemaphoreType.DMA((blocks,))], 16,
        2 * rows * block * width, 4 << 20, pinned=[*ahead, *late_far, *behind])
    total = jnp.sum(exchange(pair_sum(mine, other)).astype(F32), axis=0)
    return (mixed.astype(F32) + total).astype(BF16)


def solution(mesh):
    split = Mesh(mesh.devices.reshape(8, 2, 2, 4, 2), ("z", "xl", "xh", "y", "c"))
    in_specs = (
        P(SEQ, None),
        P(),
        P(None, SEQ, WT),
        P(SEQ, WT),
        P(),
        P(None, SEQ, WT),
        P(None, WT),
        P(WT),
        P(WT),
        P(SEQ, WT),
    )
    return jax.shard_map(local, mesh=split, in_specs=in_specs, out_specs=P(SEQ, WT), check_vma=False)
```

```python
import jax
import jax.numpy as jnp
from jax import lax
from jax.experimental import pallas as pl
from jax.experimental.pallas import tpu as pltpu
from jax.sharding import Mesh, PartitionSpec as P

HEAD_DIM = 128
BF16 = jnp.bfloat16
F32 = jnp.float32
SEQ = ("z", "xl")
WT = ("xh", "y", "c")
CHIPS = ("xh", "y")


def shift(value, axis, step):
    count = lax.axis_size(axis)
    return lax.ppermute(value, axis, [(i, (i + step) % count) for i in range(count)])


def smem():
    return pl.BlockSpec(memory_space=pltpu.SMEM)


def vmem():
    return pl.BlockSpec(memory_space=pltpu.VMEM)


def hbm():
    return pl.BlockSpec(memory_space=pltpu.HBM)


def run_kernel(body, where, arrays, outs, scratch, megabytes, flops, moved, exps=0, pinned=(), out_specs=None):
    return pl.pallas_call(
        body,
        out_shape=outs,
        in_specs=[smem()] + [vmem()] * len(arrays) + [hbm()] * len(pinned),
        out_specs=out_specs or jax.tree.map(lambda _: vmem(), outs),
        scratch_shapes=scratch,
        compiler_params=pltpu.CompilerParams(vmem_limit_bytes=megabytes << 20),
        cost_estimate=pl.CostEstimate(flops=flops, bytes_accessed=moved, transcendentals=exps),
    )(where, *arrays, *pinned)


def fetch(sources, places, sems):
    copies = [pltpu.make_async_copy(a, b, sems.at[n]) for n, (a, b) in enumerate(zip(sources, places))]
    for copy in copies:
        copy.start()
    return copies


def dot(a, b):
    return jnp.dot(a, b, preferred_element_type=F32)


def dot_t(a, b):
    return lax.dot_general(a, b, (((1,), (1,)), ((), ())), preferred_element_type=F32)


def norm_blocks_kernel(where, frames, gain, mine, other):
    rows, width = frames.shape
    blocks = mine.shape[0]
    block = mine.shape[2]
    z, xl, core = where[0], where[1], where[2]
    step_rows = 32

    def chunk(i, carry):
        r = pl.ds(pl.multiple_of(i * step_rows, step_rows), step_rows)
        wide = frames[r, :].astype(F32)
        mean = jnp.mean(wide, axis=-1, keepdims=True)
        centered = wide - mean
        scale = lax.rsqrt(jnp.mean(centered * centered, axis=-1, keepdims=True) + 1e-05)
        for out, first, parity in ((mine, 0, xl), (other, core * other.shape[0], 1 - xl)):
            for j in range(out.shape[0]):
                owner = lax.rem(z + first + j, blocks) * 2 + parity
                cols = pl.ds(pl.multiple_of(owner * block, block), block)
                part = (frames[r, cols].astype(F32) - mean) * scale * gain[:, cols]
                out[j, r, :] = part.astype(BF16)
        return carry

    lax.fori_loop(0, rows // step_rows, chunk, 0)


def project_kernel(where, mine, got, swapped, *refs):
    pieces, (kv_keep, q_keep, send, weights, sems) = refs[:-5], refs[-5:]
    xl, core = where[1], where[2]
    low = [jnp.where(core == 0, got[j], swapped[j]) for j in range(4)]
    high = [jnp.where(core == 0, swapped[j], got[j]) for j in range(4)]
    half = pieces[4].shape[1]
    places = [weights.at[:, j] for j in range(4)] + [weights.at[:, 4, :half], weights.at[:, 4, half:]] + [weights.at[:, j] for j in range(5, 8)]
    copies = {}
    for m in (1, 2, 0):
        copies[m] = fetch([piece.at[m] for piece in pieces], [place.at[m] for place in places], sems.at[m])
    for m, keep, at in ((1, kv_keep, 0), (2, kv_keep, 1), (0, q_keep, 0)):
        for copy in copies[m]:
            copy.wait()
        for r, a in enumerate((mine, low + high)):
            acc = None
            for j in range(8):
                term = dot(a[j], weights[m, j])
                acc = term if acc is None else acc + term
            even, odd = acc[:, :HEAD_DIM], acc[:, HEAD_DIM:]
            keep[at, r] = jnp.where(xl == 0, even, odd)
            send[m, r] = jnp.where(xl == 0, odd, even).astype(BF16)


def attend_kernel(where, q_keep, got, *refs):
    parts, (mine, send, scores, held, sems) = refs[:-5], refs[-5:]
    scale = HEAD_DIM ** (-0.5)
    step_rows = 128
    chunk = held.shape[2] * held.shape[3]
    count = len(parts)
    copies = fetch(parts, [held.at[j] for j in range(count)], sems)
    for copy in copies:
        copy.wait()

    def piece(j, side):
        return held[j, side].reshape(chunk, HEAD_DIM)

    for r, out in enumerate((mine, send)):
        for i in range(0, q_keep.shape[2], step_rows):
            query = (q_keep[0, r, i : i + step_rows] + got[0, 1 - r, i : i + step_rows].astype(F32)).astype(BF16)
            best = None
            for j in range(count):
                part = dot_t(query, piece(j, 0))
                scores[:, j * chunk : (j + 1) * chunk] = part
                top = jnp.max(part, axis=-1, keepdims=True)
                best = top if best is None else jnp.maximum(best, top)
            total = jnp.zeros((step_rows, 1), F32)
            acc = jnp.zeros((step_rows, HEAD_DIM), F32)
            for j in range(count):
                weights = jnp.exp((scores[:, j * chunk : (j + 1) * chunk] - best) * scale)
                total = total + jnp.sum(weights, axis=-1, keepdims=True)
                acc = acc + dot(weights.astype(BF16), piece(j, 1))
            out[i : i + step_rows, :] = (acc / total).astype(BF16)


def spread_out(inputs, pairs, places, mine, other, same):
    for (near, far), place in zip(pairs, places):
        a = dot_t(inputs, near).astype(BF16)
        b = dot_t(inputs, far).astype(BF16)
        mine[place] = jnp.where(same, a, b)
        other[place] = jnp.where(same, b, a)


def project_out_kernel(where, own, got, weight, far_weight, mine, other):
    xl = where[1]
    a, b = own[...], got[...]
    heads = jnp.concatenate([jnp.where(xl == 0, a, b), jnp.where(xl == 0, b, a)], axis=1)
    blocks, rows, block = mine.shape
    pairs = [(weight[j * block : (j + 1) * block], far_weight[j * block : (j + 1) * block]) for j in range(blocks)]
    spread_out(heads, pairs, range(blocks), mine, other, where[2] == xl)


def glu_kernel(where, mine, other, gain, *refs):
    pieces, (gated, normed, weights, sems) = refs[:-4], refs[-4:]
    blocks, rows, block = mine.shape
    copies = fetch([piece.at[:4] for piece in pieces], [weights.at[j] for j in range(blocks)], sems)
    z, xl = where[0], where[1]
    same = where[2] == xl
    step_rows = 32
    width = 2 * blocks * block

    def chunk(i, carry):
        r = pl.ds(pl.multiple_of(i * step_rows, step_rows), step_rows)
        parts = []
        for j in range(blocks):
            at = lax.rem(z + j, blocks)
            a, b = mine[at, r, :], other[at, r, :]
            parts += [jnp.where(same, a, b).astype(F32), jnp.where(same, b, a).astype(F32)]
        mean = jnp.sum(sum(parts), axis=-1, keepdims=True) / width
        square = sum((p - mean) * (p - mean) for p in parts)
        scale = lax.rsqrt(jnp.sum(square, axis=-1, keepdims=True) / width + 1e-05)
        for n, p in enumerate(parts):
            parity = xl if n % 2 == 0 else 1 - xl
            cols = pl.ds(pl.multiple_of((lax.rem(z + n // 2, blocks) * 2 + parity) * block, block), block)
            normed[n, r, :] = ((p - mean) * scale * gain[:, cols]).astype(BF16)
        return carry

    lax.fori_loop(0, rows // step_rows, chunk, 0)
    for copy in copies:
        copy.wait()
    sums = [None, None]
    for n in range(2 * blocks):
        j = n // 2
        for m in range(2):
            term = dot(normed[n], weights[j, 2 * m + n % 2])
            sums[m] = term if sums[m] is None else sums[m] + term
    gated[...] = (sums[0] * jax.nn.sigmoid(sums[1])).astype(BF16)


def conv_kernel(where, gated, before, after, taps, scale, offset, *refs):
    pieces, (mine, other, padded, activated, weights, sems) = refs[:-6], refs[-6:]
    copies = fetch([piece.at[4:] for piece in pieces], [weights.at[j] for j in range(len(pieces))], sems)
    rows = gated.shape[0]
    rim = before.shape[0]
    seq = where[0] * 2 + where[1]
    padded[:rim] = jnp.where(seq > 0, before[...].astype(F32), 0.0)
    padded[rim : rim + rows] = gated[...].astype(F32)
    padded[rim + rows :] = jnp.where(seq < where[3] - 1, after[...].astype(F32), 0.0)
    count = taps.shape[0]
    first = rim - (count - 1) // 2
    for i in range(0, rows, 32):
        acc = None
        for k in range(count):
            term = taps[k : k + 1, :] * padded[i + first + k : i + first + k + 32, :]
            acc = term if acc is None else acc + term
        v = acc * scale[...] + offset[...]
        activated[i : i + 32, :] = (v * jax.nn.sigmoid(v)).astype(BF16)
    for copy in copies:
        copy.wait()
    pairs = [(weights[j, 0], weights[j, 1]) for j in range(8)]
    places = [lax.rem(where[0] + j, 8) for j in range(8)]
    spread_out(activated[...], pairs, places, mine, other, where[2] == where[1])


def residual_kernel(where, parts, frames, mixed, copies, held, sem, sems):
    block = mixed.shape[1]
    cols = pl.ds(pl.multiple_of(where[4] * block, block), block)
    copy = pltpu.make_async_copy(frames.at[:, cols], held, sem)
    copy.start()
    total = parts[0].astype(F32)
    for j in range(1, parts.shape[0]):
        total = total + parts[j].astype(F32)
    copy.wait()
    result = (held[...].astype(F32) + total).astype(BF16)
    mixed[...] = result
    count = copies.shape[0]
    for out in fetch([mixed] * count, [copies.at[j] for j in range(count)], sems):
        out.wait()


def both_ways(right, left):
    return shift(right, "z", 1), shift(left, "z", -1)


def pair_sum(mine, other):
    got = shift(other, "c", 1)
    return (mine.astype(F32) + got.astype(F32)).astype(BF16)


def exchange(parts):
    return lax.all_to_all(parts, CHIPS, 0, 0, tiled=True)


def local(
    frames,
    attn_norm_gain,
    qkv_weight,
    attn_out_weight,
    conv_norm_gain,
    glu_weight,
    depth_kernel,
    norm_scale,
    norm_shift,
    conv_out_weight,
):
    rows, width = frames.shape
    block = qkv_weight.shape[2]
    blocks = width // block // 2
    z, xl, core = (lax.axis_index(a) for a in ("z", "xl", "c"))
    where = jnp.stack([z, xl, core, lax.axis_size(SEQ), lax.axis_index(WT)]).astype(jnp.int32)
    S = jax.ShapeDtypeStruct

    step = lax.optimization_barrier
    out_weight = lax.all_gather(attn_out_weight, "z", axis=0, tiled=True)
    late = jnp.concatenate([glu_weight, conv_out_weight[None]])
    late_far = shift(late, "xl", 1)

    half = block // 2
    r1, l1 = both_ways(qkv_weight, qkv_weight)
    mine, other = run_kernel(
        norm_blocks_kernel, where, [frames, attn_norm_gain.reshape(1, width)],
        [S((blocks, rows, block), BF16), S((blocks // 2, rows, block), BF16)], [], 16, 10 * rows * width, 4 * rows * width)
    got = shift(other, "xl", 1)
    r2, l2 = both_ways(r1, l1)
    r3, l3 = both_ways(r2, l2)
    far = both_ways(r3[:, :half], l3[:, half:])
    swapped, late_far = step((shift(got, "c", 1), late_far))
    late = jnp.stack([late, late_far], axis=1).reshape(6, block, block)
    kv_keep, q_keep, send = run_kernel(
        project_kernel, where, [mine, got, swapped],
        [S((2, 2, rows, HEAD_DIM), F32), S((1, 2, rows, HEAD_DIM), F32), S((3, 2, rows, HEAD_DIM), BF16)],
        [pltpu.VMEM((3, blocks, block, block), BF16), pltpu.SemaphoreType.DMA((3, 9))], 60,
        6 * rows * width * block, 6 * block * block * 8 + 4 * rows * width,
        pinned=[qkv_weight, l1, l2, l3, *far, r3, r2, r1])
    got, late = step((shift(send, "xl", 1), late))
    kv = (kv_keep + got[1:, ::-1].astype(F32)).astype(BF16)

    kv_r1, kv_l1 = both_ways(kv, kv)
    kv_r2, kv_l2 = both_ways(kv_r1, kv_l1)
    kv_r3, kv_l3 = both_ways(kv_r2, kv_l2)
    out_weight = [out_weight, shift(out_weight, "xl", 1)]
    kv_r3, kv_l3, late_left = step((kv_r3, kv_l3, late))
    late_l1 = shift(late_left, "z", -1)
    kv_r4, late_right = step((shift(kv_r3, "z", 1), late))
    late_r1 = shift(late_right, "z", 1)
    own, away = run_kernel(
        attend_kernel, where, [q_keep, got], [S((rows, HEAD_DIM), BF16)] * 2,
        [pltpu.VMEM((128, 16 * rows), F32), pltpu.VMEM((blocks, 2, 2, rows, HEAD_DIM), BF16), pltpu.SemaphoreType.DMA((blocks,))], 32,
        8 * rows * 16 * rows * HEAD_DIM, 4 << 20, 2 * rows * 16 * rows,
        pinned=[kv, kv_l1, kv_l2, kv_l3, kv_r4, kv_r3, kv_r2, kv_r1])
    back, late_l1 = step((shift(away, "xl", 1), late_l1))
    blocks_out = [S((blocks, rows, block), BF16)] * 2
    mine, other = run_kernel(
        project_out_kernel, where, [own, back] + out_weight, blocks_out, [], 16,
        2 * rows * block * width, 4 << 20)
    other, late_r1, late_l1 = step((other, late_r1, late_l1))
    late_r2, late_l2 = both_ways(late_r1, late_l1)
    late_r3, late_l3 = both_ways(late_r2, late_l2)
    mixed, copies = run_kernel(
        residual_kernel, where, [exchange(pair_sum(mine, other))],
        [S((rows, block), BF16), S((blocks, rows, block), BF16)],
        [pltpu.VMEM((rows, block), BF16), pltpu.SemaphoreType.DMA, pltpu.SemaphoreType.DMA((blocks,))], 16,
        10 * rows * block, 20 * rows * block, pinned=[frames], out_specs=[vmem(), hbm()])
    late_l4 = shift(late_l3, "z", -1)
    mine, late_l4, late_r3 = step((exchange(copies), late_l4, late_r3))
    other = shift(mine, "c", 1)
    late = [late, late_l1, late_l2, late_l3, late_l4, late_r3, late_r2, late_r1]
    gated = run_kernel(
        glu_kernel, where, [mine, other, conv_norm_gain.reshape(1, width)],
        S((rows, block), BF16),
        [pltpu.VMEM((2 * blocks, rows, block), BF16), pltpu.VMEM((blocks, 4, block, block), BF16), pltpu.SemaphoreType.DMA((blocks,))], 48,
        4 * rows * block * width, 6 << 20, pinned=late)
    rim = 16
    before = shift(gated[rows - rim :], SEQ, 1)
    after = shift(gated[:rim], SEQ, -1)
    mine, other = run_kernel(
        conv_kernel, where,
        [gated, before, after, depth_kernel, norm_scale.reshape(1, block), norm_shift.reshape(1, block)],
        blocks_out,
        [pltpu.VMEM((rows + 2 * rim, block), F32), pltpu.VMEM((rows, block), BF16),
         pltpu.VMEM((blocks, 2, block, block), BF16), pltpu.SemaphoreType.DMA((blocks,))], 16,
        2 * rows * block * width, 4 << 20, pinned=late)
    total = jnp.sum(exchange(pair_sum(mine, other)).astype(F32), axis=0)
    return (mixed.astype(F32) + total).astype(BF16)


def solution(mesh):
    split = Mesh(mesh.devices.reshape(8, 2, 2, 4, 2), ("z", "xl", "xh", "y", "c"))
    in_specs = (
        P(SEQ, None),
        P(),
        P(None, SEQ, WT),
        P(SEQ, WT),
        P(),
        P(None, SEQ, WT),
        P(None, WT),
        P(WT),
        P(WT),
        P(SEQ, WT),
    )
    return jax.shard_map(local, mesh=split, in_specs=in_specs, out_specs=P(SEQ, WT), check_vma=False)
```

```python
import jax
import jax.numpy as jnp
from jax import lax
from jax.experimental import pallas as pl
from jax.experimental.pallas import tpu as pltpu
from jax.sharding import Mesh, PartitionSpec as P

HEAD_DIM = 128
BF16 = jnp.bfloat16
F32 = jnp.float32
SEQ = ("z", "xl")
WT = ("xh", "y", "c")
CHIPS = ("xh", "y")


def shift(value, axis, step):
    count = lax.axis_size(axis)
    return lax.ppermute(value, axis, [(i, (i + step) % count) for i in range(count)])


def smem():
    return pl.BlockSpec(memory_space=pltpu.SMEM)


def vmem():
    return pl.BlockSpec(memory_space=pltpu.VMEM)


def hbm():
    return pl.BlockSpec(memory_space=pltpu.HBM)


def run_kernel(body, where, arrays, outs, scratch, megabytes, flops, moved, exps=0, pinned=(), out_specs=None):
    return pl.pallas_call(
        body,
        out_shape=outs,
        in_specs=[smem()] + [vmem()] * len(arrays) + [hbm()] * len(pinned),
        out_specs=out_specs or jax.tree.map(lambda _: vmem(), outs),
        scratch_shapes=scratch,
        compiler_params=pltpu.CompilerParams(vmem_limit_bytes=megabytes << 20),
        cost_estimate=pl.CostEstimate(flops=flops, bytes_accessed=moved, transcendentals=exps),
    )(where, *arrays, *pinned)


def fetch(sources, places, sems):
    copies = [pltpu.make_async_copy(a, b, sems.at[n]) for n, (a, b) in enumerate(zip(sources, places))]
    for copy in copies:
        copy.start()
    return copies


def dot(a, b):
    return jnp.dot(a, b, preferred_element_type=F32)


def dot_t(a, b):
    return lax.dot_general(a, b, (((1,), (1,)), ((), ())), preferred_element_type=F32)


def norm_blocks_kernel(where, frames, gain, mine, other):
    rows, width = frames.shape
    blocks = mine.shape[0]
    block = mine.shape[2]
    z, xl, core = where[0], where[1], where[2]
    step_rows = 32

    def chunk(i, carry):
        r = pl.ds(pl.multiple_of(i * step_rows, step_rows), step_rows)
        wide = frames[r, :].astype(F32)
        mean = jnp.mean(wide, axis=-1, keepdims=True)
        centered = wide - mean
        scale = lax.rsqrt(jnp.mean(centered * centered, axis=-1, keepdims=True) + 1e-05)
        for out, first, parity in ((mine, 0, xl), (other, core * other.shape[0], 1 - xl)):
            for j in range(out.shape[0]):
                owner = lax.rem(z + first + j, blocks) * 2 + parity
                cols = pl.ds(pl.multiple_of(owner * block, block), block)
                part = (frames[r, cols].astype(F32) - mean) * scale * gain[:, cols]
                out[j, r, :] = part.astype(BF16)
        return carry

    lax.fori_loop(0, rows // step_rows, chunk, 0)


def both_rows(mine, got, swapped, core):
    low = [jnp.where(core == 0, got[j], swapped[j]) for j in range(4)]
    high = [jnp.where(core == 0, swapped[j], got[j]) for j in range(4)]
    return mine, low + high


EARLY = (0, 1, 2, 6, 7)
LATE = (3, 4, 5)


def project_early_kernel(where, mine, got, swapped, *refs):
    pieces, (sums, weights, sems) = refs[:-3], refs[-3:]
    copies = fetch(pieces, [weights.at[n] for n in range(len(pieces))], sems)
    sides = both_rows(mine, got, swapped, where[2])
    for copy in copies:
        copy.wait()
    for m in range(3):
        for r, a in enumerate(sides):
            acc = None
            for n, j in enumerate(EARLY):
                term = dot(a[j], weights[n, m])
                acc = term if acc is None else acc + term
            sums[m, r] = acc


def project_kernel(where, mine, got, swapped, sums, *refs):
    pieces, (kv_keep, q_keep, send, weights, sems) = refs[:-5], refs[-5:]
    xl, core = where[1], where[2]
    half = pieces[1].shape[1]
    copies = fetch(pieces, [weights.at[0], weights.at[1, :, :half], weights.at[1, :, half:], weights.at[2]], sems)
    sides = both_rows(mine, got, swapped, core)
    for copy in copies:
        copy.wait()
    for m, keep, at in ((1, kv_keep, 0), (2, kv_keep, 1), (0, q_keep, 0)):
        for r, a in enumerate(sides):
            acc = sums[m, r]
            for n, j in enumerate(LATE):
                acc = acc + dot(a[j], weights[n, m])
            even, odd = acc[:, :HEAD_DIM], acc[:, HEAD_DIM:]
            keep[at, r] = jnp.where(xl == 0, even, odd)
            send[m, r] = jnp.where(xl == 0, odd, even).astype(BF16)


def attend_rows(query, held, scores):
    scale = HEAD_DIM ** (-0.5)
    count = held.shape[0]
    chunk = held.shape[2] * held.shape[3]
    best = None
    for j in range(count):
        part = dot_t(query, held[j, 0].reshape(chunk, HEAD_DIM))
        scores[:, j * chunk : (j + 1) * chunk] = part
        top = jnp.max(part, axis=-1, keepdims=True)
        best = top if best is None else jnp.maximum(best, top)
    total, acc = None, None
    for j in range(count):
        weights = jnp.exp((scores[:, j * chunk : (j + 1) * chunk] - best) * scale)
        row_sum = jnp.sum(weights, axis=-1, keepdims=True)
        term = dot(weights.astype(BF16), held[j, 1].reshape(chunk, HEAD_DIM))
        total = row_sum if total is None else total + row_sum
        acc = term if acc is None else acc + term
    return best, total, acc


def query_rows(q_keep, got, r, i, count):
    return (q_keep[0, r, i : i + count] + got[0, 1 - r, i : i + count].astype(F32)).astype(BF16)


def hold(parts, held, sems):
    copies = fetch(parts, [held.at[j] for j in range(len(parts))], sems)
    for copy in copies:
        copy.wait()


def attend_early_kernel(where, q_keep, got, *refs):
    parts, (tops, totals, sums, scores, held, sems) = refs[:-6], refs[-6:]
    step_rows = scores.shape[0]
    hold(parts, held, sems)
    for r in range(2):
        for i in range(0, q_keep.shape[2], step_rows):
            best, total, acc = attend_rows(query_rows(q_keep, got, r, i, step_rows), held, scores)
            tops[r, i : i + step_rows] = jnp.broadcast_to(best, acc.shape)
            totals[r, i : i + step_rows] = jnp.broadcast_to(total, acc.shape)
            sums[r, i : i + step_rows] = acc


def attend_kernel(where, q_keep, got, tops, totals, sums, part, mine, send, scores, held, sems):
    scale = HEAD_DIM ** (-0.5)
    step_rows = scores.shape[0]
    hold([part], held, sems)
    for r, out in enumerate((mine, send)):
        for i in range(0, q_keep.shape[2], step_rows):
            best, total, acc = attend_rows(query_rows(q_keep, got, r, i, step_rows), held, scores)
            before = tops[r, i : i + step_rows]
            top = jnp.maximum(before, best)
            old, new = jnp.exp((before - top) * scale), jnp.exp((best - top) * scale)
            total = totals[r, i : i + step_rows] * old + total * new
            out[i : i + step_rows, :] = ((sums[r, i : i + step_rows] * old + acc * new) / total).astype(BF16)


def spread_out(inputs, pairs, places, mine, other, same):
    for (near, far), place in zip(pairs, places):
        a = dot_t(inputs, near).astype(BF16)
        b = dot_t(inputs, far).astype(BF16)
        mine[place] = jnp.where(same, a, b)
        other[place] = jnp.where(same, b, a)


def project_out_kernel(where, own, got, weight, far_weight, mine, other):
    xl = where[1]
    a, b = own[...], got[...]
    heads = jnp.concatenate([jnp.where(xl == 0, a, b), jnp.where(xl == 0, b, a)], axis=1)
    blocks, rows, block = mine.shape
    pairs = [(weight[j * block : (j + 1) * block], far_weight[j * block : (j + 1) * block]) for j in range(blocks)]
    spread_out(heads, pairs, range(blocks), mine, other, where[2] == xl)


def glu_kernel(where, mine, other, gain, *refs):
    pieces, (gated, normed, weights, sems) = refs[:-4], refs[-4:]
    blocks, rows, block = mine.shape
    copies = fetch([piece.at[:4] for piece in pieces], [weights.at[j] for j in range(blocks)], sems)
    z, xl = where[0], where[1]
    same = where[2] == xl
    step_rows = 32
    width = 2 * blocks * block

    def chunk(i, carry):
        r = pl.ds(pl.multiple_of(i * step_rows, step_rows), step_rows)
        parts = []
        for j in range(blocks):
            at = lax.rem(z + j, blocks)
            a, b = mine[at, r, :], other[at, r, :]
            parts += [jnp.where(same, a, b).astype(F32), jnp.where(same, b, a).astype(F32)]
        mean = jnp.sum(sum(parts), axis=-1, keepdims=True) / width
        square = sum((p - mean) * (p - mean) for p in parts)
        scale = lax.rsqrt(jnp.sum(square, axis=-1, keepdims=True) / width + 1e-05)
        for n, p in enumerate(parts):
            parity = xl if n % 2 == 0 else 1 - xl
            cols = pl.ds(pl.multiple_of((lax.rem(z + n // 2, blocks) * 2 + parity) * block, block), block)
            normed[n, r, :] = ((p - mean) * scale * gain[:, cols]).astype(BF16)
        return carry

    lax.fori_loop(0, rows // step_rows, chunk, 0)
    for copy in copies:
        copy.wait()
    sums = [None, None]
    for n in range(2 * blocks):
        j = n // 2
        for m in range(2):
            term = dot(normed[n], weights[j, 2 * m + n % 2])
            sums[m] = term if sums[m] is None else sums[m] + term
    gated[...] = (sums[0] * jax.nn.sigmoid(sums[1])).astype(BF16)


def conv_kernel(where, gated, before, after, taps, scale, offset, *refs):
    pieces, (mine, other, padded, activated, weights, sems) = refs[:-6], refs[-6:]
    copies = fetch([piece.at[4:] for piece in pieces], [weights.at[j] for j in range(len(pieces))], sems)
    rows = gated.shape[0]
    rim = before.shape[0]
    seq = where[0] * 2 + where[1]
    padded[:rim] = jnp.where(seq > 0, before[...].astype(F32), 0.0)
    padded[rim : rim + rows] = gated[...].astype(F32)
    padded[rim + rows :] = jnp.where(seq < where[3] - 1, after[...].astype(F32), 0.0)
    count = taps.shape[0]
    first = rim - (count - 1) // 2
    for i in range(0, rows, 32):
        acc = None
        for k in range(count):
            term = taps[k : k + 1, :] * padded[i + first + k : i + first + k + 32, :]
            acc = term if acc is None else acc + term
        v = acc * scale[...] + offset[...]
        activated[i : i + 32, :] = (v * jax.nn.sigmoid(v)).astype(BF16)
    for copy in copies:
        copy.wait()
    pairs = [(weights[j, 0], weights[j, 1]) for j in range(8)]
    places = [lax.rem(where[0] + j, 8) for j in range(8)]
    spread_out(activated[...], pairs, places, mine, other, where[2] == where[1])


def residual_kernel(where, parts, frames, mixed, copies, held, sem, sems):
    block = mixed.shape[1]
    cols = pl.ds(pl.multiple_of(where[4] * block, block), block)
    copy = pltpu.make_async_copy(frames.at[:, cols], held, sem)
    copy.start()
    total = parts[0].astype(F32)
    for j in range(1, parts.shape[0]):
        total = total + parts[j].astype(F32)
    copy.wait()
    result = (held[...].astype(F32) + total).astype(BF16)
    mixed[...] = result
    count = copies.shape[0]
    for out in fetch([mixed] * count, [copies.at[j] for j in range(count)], sems):
        out.wait()


def both_ways(right, left):
    return shift(right, "z", 1), shift(left, "z", -1)


def pair_sum(mine, other):
    got = shift(other, "c", 1)
    return (mine.astype(F32) + got.astype(F32)).astype(BF16)


def exchange(parts):
    return lax.all_to_all(parts, CHIPS, 0, 0, tiled=True)


def local(
    frames,
    attn_norm_gain,
    qkv_weight,
    attn_out_weight,
    conv_norm_gain,
    glu_weight,
    depth_kernel,
    norm_scale,
    norm_shift,
    conv_out_weight,
):
    rows, width = frames.shape
    block = qkv_weight.shape[2]
    blocks = width // block // 2
    z, xl, core = (lax.axis_index(a) for a in ("z", "xl", "c"))
    where = jnp.stack([z, xl, core, lax.axis_size(SEQ), lax.axis_index(WT)]).astype(jnp.int32)
    S = jax.ShapeDtypeStruct

    step = lax.optimization_barrier
    out_weight = lax.all_gather(attn_out_weight, "z", axis=0, tiled=True)
    late = jnp.concatenate([glu_weight, conv_out_weight[None]])
    late_far = shift(late, "xl", 1)

    half = block // 2
    r1, l1 = both_ways(qkv_weight, qkv_weight)
    mine, other = run_kernel(
        norm_blocks_kernel, where, [frames, attn_norm_gain.reshape(1, width)],
        [S((blocks, rows, block), BF16), S((blocks // 2, rows, block), BF16)], [], 16, 10 * rows * width, 4 * rows * width)
    got = shift(other, "xl", 1)
    r2, l2 = both_ways(r1, l1)
    r3, l3 = both_ways(r2, l2)
    far = both_ways(r3[:, :half], l3[:, half:])
    swapped, late_far = step((shift(got, "c", 1), late_far))
    late = jnp.stack([late, late_far], axis=1).reshape(6, block, block)
    sums = run_kernel(
        project_early_kernel, where, [mine, got, swapped], S((3, 2, rows, block), F32),
        [pltpu.VMEM((len(EARLY), 3, block, block), BF16), pltpu.SemaphoreType.DMA((len(EARLY),))], 60,
        4 * rows * width * block, 6 << 20, pinned=[qkv_weight, l1, l2, r2, r1])
    kv_keep, q_keep, send = run_kernel(
        project_kernel, where, [mine, got, swapped, sums],
        [S((2, 2, rows, HEAD_DIM), F32), S((1, 2, rows, HEAD_DIM), F32), S((3, 2, rows, HEAD_DIM), BF16)],
        [pltpu.VMEM((len(LATE), 3, block, block), BF16), pltpu.SemaphoreType.DMA((4,))], 60,
        2 * rows * width * block, 6 << 20, pinned=[l3, *far, r3])
    got, late = step((shift(send, "xl", 1), late))
    kv = (kv_keep + got[1:, ::-1].astype(F32)).astype(BF16)

    kv_r1, kv_l1 = both_ways(kv, kv)
    kv_r2, kv_l2 = both_ways(kv_r1, kv_l1)
    kv_r3, kv_l3 = both_ways(kv_r2, kv_l2)
    out_weight = [out_weight, shift(out_weight, "xl", 1)]
    kv_r3, kv_l3, late_left = step((kv_r3, kv_l3, late))
    late_l1 = shift(late_left, "z", -1)
    kv_r4 = shift(kv_r3, "z", 1)
    parts = [kv, kv_l1, kv_l2, kv_l3, kv_r3, kv_r2, kv_r1]
    stat = S((2, rows, HEAD_DIM), F32)

    def attend_scratch(count):
        return [pltpu.VMEM((128, 2 * rows * count), F32), pltpu.VMEM((count, 2, 2, rows, HEAD_DIM), BF16), pltpu.SemaphoreType.DMA((count,))]

    tops, totals, sums = run_kernel(
        attend_early_kernel, where, [q_keep, got], [stat] * 3, attend_scratch(len(parts)), 32,
        7 * rows * 16 * rows * HEAD_DIM, 4 << 20, 2 * rows * 14 * rows, pinned=parts)
    kv_r4, late_right, tops, totals, sums = step((kv_r4, late, tops, totals, sums))
    late_r1 = shift(late_right, "z", 1)
    own, away = run_kernel(
        attend_kernel, where, [q_keep, got, tops, totals, sums], [S((rows, HEAD_DIM), BF16)] * 2, attend_scratch(1), 32,
        rows * 16 * rows * HEAD_DIM, 2 << 20, 2 * rows * 2 * rows, pinned=[kv_r4])
    back, late_l1 = step((shift(away, "xl", 1), late_l1))
    blocks_out = [S((blocks, rows, block), BF16)] * 2
    mine, other = run_kernel(
        project_out_kernel, where, [own, back] + out_weight, blocks_out, [], 16,
        2 * rows * block * width, 4 << 20)
    other, late_r1, late_l1 = step((other, late_r1, late_l1))
    late_r2, late_l2 = both_ways(late_r1, late_l1)
    late_r3, late_l3 = both_ways(late_r2, late_l2)
    mixed, copies = run_kernel(
        residual_kernel, where, [exchange(pair_sum(mine, other))],
        [S((rows, block), BF16), S((blocks, rows, block), BF16)],
        [pltpu.VMEM((rows, block), BF16), pltpu.SemaphoreType.DMA, pltpu.SemaphoreType.DMA((blocks,))], 16,
        10 * rows * block, 20 * rows * block, pinned=[frames], out_specs=[vmem(), hbm()])
    late_l4 = shift(late_l3, "z", -1)
    mine, late_l4, late_r3 = step((exchange(copies), late_l4, late_r3))
    other = shift(mine, "c", 1)
    late = [late, late_l1, late_l2, late_l3, late_l4, late_r3, late_r2, late_r1]
    gated = run_kernel(
        glu_kernel, where, [mine, other, conv_norm_gain.reshape(1, width)],
        S((rows, block), BF16),
        [pltpu.VMEM((2 * blocks, rows, block), BF16), pltpu.VMEM((blocks, 4, block, block), BF16), pltpu.SemaphoreType.DMA((blocks,))], 48,
        4 * rows * block * width, 6 << 20, pinned=late)
    rim = 16
    before = shift(gated[rows - rim :], SEQ, 1)
    after = shift(gated[:rim], SEQ, -1)
    mine, other = run_kernel(
        conv_kernel, where,
        [gated, before, after, depth_kernel, norm_scale.reshape(1, block), norm_shift.reshape(1, block)],
        blocks_out,
        [pltpu.VMEM((rows + 2 * rim, block), F32), pltpu.VMEM((rows, block), BF16),
         pltpu.VMEM((blocks, 2, block, block), BF16), pltpu.SemaphoreType.DMA((blocks,))], 16,
        2 * rows * block * width, 4 << 20, pinned=late)
    total = jnp.sum(exchange(pair_sum(mine, other)).astype(F32), axis=0)
    return (mixed.astype(F32) + total).astype(BF16)


def solution(mesh):
    split = Mesh(mesh.devices.reshape(8, 2, 2, 4, 2), ("z", "xl", "xh", "y", "c"))
    in_specs = (
        P(SEQ, None),
        P(),
        P(None, SEQ, WT),
        P(SEQ, WT),
        P(),
        P(None, SEQ, WT),
        P(None, WT),
        P(WT),
        P(WT),
        P(SEQ, WT),
    )
    return jax.shard_map(local, mesh=split, in_specs=in_specs, out_specs=P(SEQ, WT), check_vma=False)
```

```python
import jax
import jax.numpy as jnp
from jax import lax
from jax.experimental import pallas as pl
from jax.experimental.pallas import tpu as pltpu
from jax.sharding import Mesh, PartitionSpec as P

HEAD_DIM = 128
BF16 = jnp.bfloat16
F32 = jnp.float32
SEQ = ("z", "xl")
WT = ("xh", "y", "c")
CHIPS = ("xh", "y")


def shift(value, axis, step):
    count = lax.axis_size(axis)
    return lax.ppermute(value, axis, [(i, (i + step) % count) for i in range(count)])


def smem():
    return pl.BlockSpec(memory_space=pltpu.SMEM)


def vmem():
    return pl.BlockSpec(memory_space=pltpu.VMEM)


def hbm():
    return pl.BlockSpec(memory_space=pltpu.HBM)


def run_kernel(body, where, arrays, outs, scratch, megabytes, flops, moved, exps=0, pinned=(), out_specs=None):
    return pl.pallas_call(
        body,
        out_shape=outs,
        in_specs=[smem()] + [vmem()] * len(arrays) + [hbm()] * len(pinned),
        out_specs=out_specs or jax.tree.map(lambda _: vmem(), outs),
        scratch_shapes=scratch,
        compiler_params=pltpu.CompilerParams(vmem_limit_bytes=megabytes << 20),
        cost_estimate=pl.CostEstimate(flops=flops, bytes_accessed=moved, transcendentals=exps),
    )(where, *arrays, *pinned)


def fetch(sources, places, sems):
    copies = [pltpu.make_async_copy(a, b, sems.at[n]) for n, (a, b) in enumerate(zip(sources, places))]
    for copy in copies:
        copy.start()
    return copies


def dot(a, b):
    return jnp.dot(a, b, preferred_element_type=F32)


def dot_t(a, b):
    return lax.dot_general(a, b, (((1,), (1,)), ((), ())), preferred_element_type=F32)


def norm_blocks_kernel(where, frames, gain, mine, other):
    rows, width = frames.shape
    blocks = mine.shape[0]
    block = mine.shape[2]
    z, xl, core = where[0], where[1], where[2]
    step_rows = 32

    def chunk(i, carry):
        r = pl.ds(pl.multiple_of(i * step_rows, step_rows), step_rows)
        wide = frames[r, :].astype(F32)
        mean = jnp.mean(wide, axis=-1, keepdims=True)
        centered = wide - mean
        scale = lax.rsqrt(jnp.mean(centered * centered, axis=-1, keepdims=True) + 1e-05)
        for out, first, parity in ((mine, 0, xl), (other, core * other.shape[0], 1 - xl)):
            for j in range(out.shape[0]):
                owner = lax.rem(z + first + j, blocks) * 2 + parity
                cols = pl.ds(pl.multiple_of(owner * block, block), block)
                part = (frames[r, cols].astype(F32) - mean) * scale * gain[:, cols]
                out[j, r, :] = part.astype(BF16)
        return carry

    lax.fori_loop(0, rows // step_rows, chunk, 0)


def project_kernel(where, mine, got, swapped, *refs):
    pieces, (kv_keep, q_keep, send, weights, sems) = refs[:-5], refs[-5:]
    xl, core = where[1], where[2]
    low = [jnp.where(core == 0, got[j], swapped[j]) for j in range(4)]
    high = [jnp.where(core == 0, swapped[j], got[j]) for j in range(4)]
    half = pieces[4].shape[1]
    places = [weights.at[:, j] for j in range(4)] + [weights.at[:, 4, :half], weights.at[:, 4, half:]] + [weights.at[:, j] for j in range(5, 8)]
    copies = {}
    for m in (1, 2, 0):
        copies[m] = fetch([piece.at[m] for piece in pieces], [place.at[m] for place in places], sems.at[m])
    for m, keep, at in ((1, kv_keep, 0), (2, kv_keep, 1), (0, q_keep, 0)):
        for copy in copies[m]:
            copy.wait()
        for r, a in enumerate((mine, low + high)):
            acc = None
            for j in range(8):
                term = dot(a[j], weights[m, j])
                acc = term if acc is None else acc + term
            even, odd = acc[:, :HEAD_DIM], acc[:, HEAD_DIM:]
            keep[at, r] = jnp.where(xl == 0, even, odd)
            send[m, r] = jnp.where(xl == 0, odd, even).astype(BF16)


def attend_rows(query, held, scores):
    scale = HEAD_DIM ** (-0.5)
    count = held.shape[0]
    chunk = held.shape[2] * held.shape[3]
    best = None
    for j in range(count):
        part = dot_t(query, held[j, 0].reshape(chunk, HEAD_DIM))
        scores[:, j * chunk : (j + 1) * chunk] = part
        top = jnp.max(part, axis=-1, keepdims=True)
        best = top if best is None else jnp.maximum(best, top)
    total, acc = None, None
    for j in range(count):
        weights = jnp.exp((scores[:, j * chunk : (j + 1) * chunk] - best) * scale)
        row_sum = jnp.sum(weights, axis=-1, keepdims=True)
        term = dot(weights.astype(BF16), held[j, 1].reshape(chunk, HEAD_DIM))
        total = row_sum if total is None else total + row_sum
        acc = term if acc is None else acc + term
    return best, total, acc


def query_rows(q_keep, got, r, i, count):
    return (q_keep[0, r, i : i + count] + got[0, 1 - r, i : i + count].astype(F32)).astype(BF16)


def hold(parts, held, sems):
    copies = fetch(parts, [held.at[j] for j in range(len(parts))], sems)
    for copy in copies:
        copy.wait()


def attend_early_kernel(where, q_keep, got, *refs):
    parts, (tops, totals, sums, scores, held, sems) = refs[:-6], refs[-6:]
    step_rows = scores.shape[0]
    hold(parts, held, sems)
    for r in range(2):
        for i in range(0, q_keep.shape[2], step_rows):
            best, total, acc = attend_rows(query_rows(q_keep, got, r, i, step_rows), held, scores)
            tops[r, i : i + step_rows] = jnp.broadcast_to(best, acc.shape)
            totals[r, i : i + step_rows] = jnp.broadcast_to(total, acc.shape)
            sums[r, i : i + step_rows] = acc


def attend_kernel(where, q_keep, got, tops, totals, sums, part, mine, send, scores, held, sems):
    scale = HEAD_DIM ** (-0.5)
    step_rows = scores.shape[0]
    hold([part], held, sems)
    for r, out in enumerate((mine, send)):
        for i in range(0, q_keep.shape[2], step_rows):
            best, total, acc = attend_rows(query_rows(q_keep, got, r, i, step_rows), held, scores)
            before = tops[r, i : i + step_rows]
            top = jnp.maximum(before, best)
            old, new = jnp.exp((before - top) * scale), jnp.exp((best - top) * scale)
            total = totals[r, i : i + step_rows] * old + total * new
            out[i : i + step_rows, :] = ((sums[r, i : i + step_rows] * old + acc * new) / total).astype(BF16)


def spread_out(inputs, pairs, places, mine, other, same):
    for (near, far), place in zip(pairs, places):
        a = dot_t(inputs, near).astype(BF16)
        b = dot_t(inputs, far).astype(BF16)
        mine[place] = jnp.where(same, a, b)
        other[place] = jnp.where(same, b, a)


def project_out_kernel(where, own, got, weight, far_weight, mine, other):
    xl = where[1]
    a, b = own[...], got[...]
    heads = jnp.concatenate([jnp.where(xl == 0, a, b), jnp.where(xl == 0, b, a)], axis=1)
    blocks, rows, block = mine.shape
    pairs = [(weight[j * block : (j + 1) * block], far_weight[j * block : (j + 1) * block]) for j in range(blocks)]
    spread_out(heads, pairs, range(blocks), mine, other, where[2] == xl)


def glu_kernel(where, mine, other, gain, *refs):
    pieces, (gated, normed, weights, sems) = refs[:-4], refs[-4:]
    blocks, rows, block = mine.shape
    copies = fetch([piece.at[:4] for piece in pieces], [weights.at[j] for j in range(blocks)], sems)
    z, xl = where[0], where[1]
    same = where[2] == xl
    step_rows = 32
    width = 2 * blocks * block

    def chunk(i, carry):
        r = pl.ds(pl.multiple_of(i * step_rows, step_rows), step_rows)
        parts = []
        for j in range(blocks):
            at = lax.rem(z + j, blocks)
            a, b = mine[at, r, :], other[at, r, :]
            parts += [jnp.where(same, a, b).astype(F32), jnp.where(same, b, a).astype(F32)]
        mean = jnp.sum(sum(parts), axis=-1, keepdims=True) / width
        square = sum((p - mean) * (p - mean) for p in parts)
        scale = lax.rsqrt(jnp.sum(square, axis=-1, keepdims=True) / width + 1e-05)
        for n, p in enumerate(parts):
            parity = xl if n % 2 == 0 else 1 - xl
            cols = pl.ds(pl.multiple_of((lax.rem(z + n // 2, blocks) * 2 + parity) * block, block), block)
            normed[n, r, :] = ((p - mean) * scale * gain[:, cols]).astype(BF16)
        return carry

    lax.fori_loop(0, rows // step_rows, chunk, 0)
    for copy in copies:
        copy.wait()
    sums = [None, None]
    for n in range(2 * blocks):
        j = n // 2
        for m in range(2):
            term = dot(normed[n], weights[j, 2 * m + n % 2])
            sums[m] = term if sums[m] is None else sums[m] + term
    gated[...] = (sums[0] * jax.nn.sigmoid(sums[1])).astype(BF16)


def conv_kernel(where, gated, before, after, taps, scale, offset, *refs):
    pieces, (mine, other, padded, activated, weights, sems) = refs[:-6], refs[-6:]
    copies = fetch([piece.at[4:] for piece in pieces], [weights.at[j] for j in range(len(pieces))], sems)
    rows = gated.shape[0]
    rim = before.shape[0]
    seq = where[0] * 2 + where[1]
    padded[:rim] = jnp.where(seq > 0, before[...].astype(F32), 0.0)
    padded[rim : rim + rows] = gated[...].astype(F32)
    padded[rim + rows :] = jnp.where(seq < where[3] - 1, after[...].astype(F32), 0.0)
    count = taps.shape[0]
    first = rim - (count - 1) // 2
    for i in range(0, rows, 32):
        acc = None
        for k in range(count):
            term = taps[k : k + 1, :] * padded[i + first + k : i + first + k + 32, :]
            acc = term if acc is None else acc + term
        v = acc * scale[...] + offset[...]
        activated[i : i + 32, :] = (v * jax.nn.sigmoid(v)).astype(BF16)
    for copy in copies:
        copy.wait()
    pairs = [(weights[j, 0], weights[j, 1]) for j in range(8)]
    places = [lax.rem(where[0] + j, 8) for j in range(8)]
    spread_out(activated[...], pairs, places, mine, other, where[2] == where[1])


def residual_kernel(where, parts, frames, mixed, copies, held, sem, sems):
    block = mixed.shape[1]
    cols = pl.ds(pl.multiple_of(where[4] * block, block), block)
    copy = pltpu.make_async_copy(frames.at[:, cols], held, sem)
    copy.start()
    total = parts[0].astype(F32)
    for j in range(1, parts.shape[0]):
        total = total + parts[j].astype(F32)
    copy.wait()
    result = (held[...].astype(F32) + total).astype(BF16)
    mixed[...] = result
    count = copies.shape[0]
    for out in fetch([mixed] * count, [copies.at[j] for j in range(count)], sems):
        out.wait()


def both_ways(right, left):
    return shift(right, "z", 1), shift(left, "z", -1)


def pair_sum(mine, other):
    got = shift(other, "c", 1)
    return (mine.astype(F32) + got.astype(F32)).astype(BF16)


def exchange(parts):
    return lax.all_to_all(parts, CHIPS, 0, 0, tiled=True)


def local(
    frames,
    attn_norm_gain,
    qkv_weight,
    attn_out_weight,
    conv_norm_gain,
    glu_weight,
    depth_kernel,
    norm_scale,
    norm_shift,
    conv_out_weight,
):
    rows, width = frames.shape
    block = qkv_weight.shape[2]
    blocks = width // block // 2
    z, xl, core = (lax.axis_index(a) for a in ("z", "xl", "c"))
    where = jnp.stack([z, xl, core, lax.axis_size(SEQ), lax.axis_index(WT)]).astype(jnp.int32)
    S = jax.ShapeDtypeStruct

    step = lax.optimization_barrier
    out_weight = lax.all_gather(attn_out_weight, "z", axis=0, tiled=True)
    late = jnp.concatenate([glu_weight, conv_out_weight[None]])
    late_far = shift(late, "xl", 1)

    half = block // 2
    r1, l1 = both_ways(qkv_weight, qkv_weight)
    mine, other = run_kernel(
        norm_blocks_kernel, where, [frames, attn_norm_gain.reshape(1, width)],
        [S((blocks, rows, block), BF16), S((blocks // 2, rows, block), BF16)], [], 16, 10 * rows * width, 4 * rows * width)
    got = shift(other, "xl", 1)
    r2, l2 = both_ways(r1, l1)
    r3, l3 = both_ways(r2, l2)
    far = both_ways(r3[:, :half], l3[:, half:])
    swapped, late_far = step((shift(got, "c", 1), late_far))
    late = jnp.stack([late, late_far], axis=1).reshape(6, block, block)
    kv_keep, q_keep, send = run_kernel(
        project_kernel, where, [mine, got, swapped],
        [S((2, 2, rows, HEAD_DIM), F32), S((1, 2, rows, HEAD_DIM), F32), S((3, 2, rows, HEAD_DIM), BF16)],
        [pltpu.VMEM((3, blocks, block, block), BF16), pltpu.SemaphoreType.DMA((3, 9))], 60,
        6 * rows * width * block, 6 * block * block * 8 + 4 * rows * width,
        pinned=[qkv_weight, l1, l2, l3, *far, r3, r2, r1])
    got, late = step((shift(send, "xl", 1), late))
    kv = (kv_keep + got[1:, ::-1].astype(F32)).astype(BF16)

    kv_r1, kv_l1 = both_ways(kv, kv)
    kv_r2, kv_l2 = both_ways(kv_r1, kv_l1)
    kv_r3, kv_l3 = both_ways(kv_r2, kv_l2)
    out_weight = [out_weight, shift(out_weight, "xl", 1)]
    kv_r3, kv_l3, late_left = step((kv_r3, kv_l3, late))
    late_l1 = shift(late_left, "z", -1)
    kv_r4 = shift(kv_r3, "z", 1)
    parts = [kv, kv_l1, kv_l2, kv_l3, kv_r3, kv_r2, kv_r1]
    stat = S((2, rows, HEAD_DIM), F32)

    def attend_scratch(count):
        return [pltpu.VMEM((128, 2 * rows * count), F32), pltpu.VMEM((count, 2, 2, rows, HEAD_DIM), BF16), pltpu.SemaphoreType.DMA((count,))]

    tops, totals, sums = run_kernel(
        attend_early_kernel, where, [q_keep, got], [stat] * 3, attend_scratch(len(parts)), 32,
        7 * rows * 16 * rows * HEAD_DIM, 4 << 20, 2 * rows * 14 * rows, pinned=parts)
    kv_r4, late_right, tops, totals, sums = step((kv_r4, late, tops, totals, sums))
    late_r1 = shift(late_right, "z", 1)
    own, away = run_kernel(
        attend_kernel, where, [q_keep, got, tops, totals, sums], [S((rows, HEAD_DIM), BF16)] * 2, attend_scratch(1), 32,
        rows * 16 * rows * HEAD_DIM, 2 << 20, 2 * rows * 2 * rows, pinned=[kv_r4])
    back, late_l1 = step((shift(away, "xl", 1), late_l1))
    blocks_out = [S((blocks, rows, block), BF16)] * 2
    mine, other = run_kernel(
        project_out_kernel, where, [own, back] + out_weight, blocks_out, [], 16,
        2 * rows * block * width, 4 << 20)
    other, late_r1 = step((other, late_r1))
    late_r2, late_l2 = both_ways(late_r1, late_l1)
    late_r3, late_l3 = both_ways(late_r2, late_l2)
    mixed, copies = run_kernel(
        residual_kernel, where, [exchange(pair_sum(mine, other))],
        [S((rows, block), BF16), S((blocks, rows, block), BF16)],
        [pltpu.VMEM((rows, block), BF16), pltpu.SemaphoreType.DMA, pltpu.SemaphoreType.DMA((blocks,))], 16,
        10 * rows * block, 20 * rows * block, pinned=[frames], out_specs=[vmem(), hbm()])
    late_l4 = shift(late_l3, "z", -1)
    mine, late_l4, late_r3 = step((exchange(copies), late_l4, late_r3))
    other = shift(mine, "c", 1)
    late = [late, late_l1, late_l2, late_l3, late_l4, late_r3, late_r2, late_r1]
    gated = run_kernel(
        glu_kernel, where, [mine, other, conv_norm_gain.reshape(1, width)],
        S((rows, block), BF16),
        [pltpu.VMEM((2 * blocks, rows, block), BF16), pltpu.VMEM((blocks, 4, block, block), BF16), pltpu.SemaphoreType.DMA((blocks,))], 48,
        4 * rows * block * width, 6 << 20, pinned=late)
    rim = 16
    before = shift(gated[rows - rim :], SEQ, 1)
    after = shift(gated[:rim], SEQ, -1)
    mine, other = run_kernel(
        conv_kernel, where,
        [gated, before, after, depth_kernel, norm_scale.reshape(1, block), norm_shift.reshape(1, block)],
        blocks_out,
        [pltpu.VMEM((rows + 2 * rim, block), F32), pltpu.VMEM((rows, block), BF16),
         pltpu.VMEM((blocks, 2, block, block), BF16), pltpu.SemaphoreType.DMA((blocks,))], 16,
        2 * rows * block * width, 4 << 20, pinned=late)
    total = jnp.sum(exchange(pair_sum(mine, other)).astype(F32), axis=0)
    return (mixed.astype(F32) + total).astype(BF16)


def solution(mesh):
    split = Mesh(mesh.devices.reshape(8, 2, 2, 4, 2), ("z", "xl", "xh", "y", "c"))
    in_specs = (
        P(SEQ, None),
        P(),
        P(None, SEQ, WT),
        P(SEQ, WT),
        P(),
        P(None, SEQ, WT),
        P(None, WT),
        P(WT),
        P(WT),
        P(SEQ, WT),
    )
    return jax.shard_map(local, mesh=split, in_specs=in_specs, out_specs=P(SEQ, WT), check_vma=False)
```

```python
import jax
import jax.numpy as jnp
from jax import lax
from jax.experimental import pallas as pl
from jax.experimental.pallas import tpu as pltpu
from jax.sharding import Mesh, PartitionSpec as P

HEAD_DIM = 128
BF16 = jnp.bfloat16
F32 = jnp.float32
SEQ = ("z", "xl")
WT = ("xh", "y", "c")
CHIPS = ("xh", "y")


def shift(value, axis, step):
    count = lax.axis_size(axis)
    return lax.ppermute(value, axis, [(i, (i + step) % count) for i in range(count)])


def smem():
    return pl.BlockSpec(memory_space=pltpu.SMEM)


def vmem():
    return pl.BlockSpec(memory_space=pltpu.VMEM)


def hbm():
    return pl.BlockSpec(memory_space=pltpu.HBM)


def run_kernel(body, where, arrays, outs, scratch, megabytes, flops, moved, exps=0, pinned=(), out_specs=None):
    return pl.pallas_call(
        body,
        out_shape=outs,
        in_specs=[smem()] + [vmem()] * len(arrays) + [hbm()] * len(pinned),
        out_specs=out_specs or jax.tree.map(lambda _: vmem(), outs),
        scratch_shapes=scratch,
        compiler_params=pltpu.CompilerParams(vmem_limit_bytes=megabytes << 20),
        cost_estimate=pl.CostEstimate(flops=flops, bytes_accessed=moved, transcendentals=exps),
    )(where, *arrays, *pinned)


def fetch(sources, places, sems):
    copies = [pltpu.make_async_copy(a, b, sems.at[n]) for n, (a, b) in enumerate(zip(sources, places))]
    for copy in copies:
        copy.start()
    return copies


def dot(a, b):
    return jnp.dot(a, b, preferred_element_type=F32)


def dot_t(a, b):
    return lax.dot_general(a, b, (((1,), (1,)), ((), ())), preferred_element_type=F32)


def norm_blocks_kernel(where, frames, gain, mine, other):
    rows, width = frames.shape
    blocks = mine.shape[0]
    block = mine.shape[2]
    z, xl, core = where[0], where[1], where[2]
    step_rows = 32

    def chunk(i, carry):
        r = pl.ds(pl.multiple_of(i * step_rows, step_rows), step_rows)
        wide = frames[r, :].astype(F32)
        mean = jnp.mean(wide, axis=-1, keepdims=True)
        centered = wide - mean
        scale = lax.rsqrt(jnp.mean(centered * centered, axis=-1, keepdims=True) + 1e-05)
        for out, first, parity in ((mine, 0, xl), (other, core * other.shape[0], 1 - xl)):
            for j in range(out.shape[0]):
                owner = lax.rem(z + first + j, blocks) * 2 + parity
                cols = pl.ds(pl.multiple_of(owner * block, block), block)
                part = (frames[r, cols].astype(F32) - mean) * scale * gain[:, cols]
                out[j, r, :] = part.astype(BF16)
        return carry

    lax.fori_loop(0, rows // step_rows, chunk, 0)


def project_kernel(where, mine, got, swapped, *refs):
    pieces, (kv_keep, q_keep, send, weights, sems) = refs[:-5], refs[-5:]
    xl, core = where[1], where[2]
    low = [jnp.where(core == 0, got[j], swapped[j]) for j in range(4)]
    high = [jnp.where(core == 0, swapped[j], got[j]) for j in range(4)]
    half = pieces[4].shape[1]
    places = [weights.at[:, j] for j in range(4)] + [weights.at[:, 4, :half], weights.at[:, 4, half:]] + [weights.at[:, j] for j in range(5, 8)]
    copies = {}
    for m in (1, 2, 0):
        copies[m] = fetch([piece.at[m] for piece in pieces], [place.at[m] for place in places], sems.at[m])
    for m, keep, at in ((1, kv_keep, 0), (2, kv_keep, 1), (0, q_keep, 0)):
        for copy in copies[m]:
            copy.wait()
        for r, a in enumerate((mine, low + high)):
            acc = None
            for j in range(8):
                term = dot(a[j], weights[m, j])
                acc = term if acc is None else acc + term
            even, odd = acc[:, :HEAD_DIM], acc[:, HEAD_DIM:]
            keep[at, r] = jnp.where(xl == 0, even, odd)
            send[m, r] = jnp.where(xl == 0, odd, even).astype(BF16)


def attend_rows(query, held, scores):
    scale = HEAD_DIM ** (-0.5)
    count = held.shape[0]
    chunk = held.shape[2] * held.shape[3]
    best = None
    for j in range(count):
        part = dot_t(query, held[j, 0].reshape(chunk, HEAD_DIM))
        scores[:, j * chunk : (j + 1) * chunk] = part
        top = jnp.max(part, axis=-1, keepdims=True)
        best = top if best is None else jnp.maximum(best, top)
    total, acc = None, None
    for j in range(count):
        weights = jnp.exp((scores[:, j * chunk : (j + 1) * chunk] - best) * scale)
        row_sum = jnp.sum(weights, axis=-1, keepdims=True)
        term = dot(weights.astype(BF16), held[j, 1].reshape(chunk, HEAD_DIM))
        total = row_sum if total is None else total + row_sum
        acc = term if acc is None else acc + term
    return best, total, acc


def query_rows(q_keep, got, r, i, count):
    return (q_keep[0, r, i : i + count] + got[0, 1 - r, i : i + count].astype(F32)).astype(BF16)


def hold(parts, held, sems):
    copies = fetch(parts, [held.at[j] for j in range(len(parts))], sems)
    for copy in copies:
        copy.wait()


def attend_early_kernel(where, q_keep, got, *refs):
    parts, (tops, totals, sums, scores, held, sems) = refs[:-6], refs[-6:]
    step_rows = scores.shape[0]
    hold(parts, held, sems)
    for r in range(2):
        for i in range(0, q_keep.shape[2], step_rows):
            best, total, acc = attend_rows(query_rows(q_keep, got, r, i, step_rows), held, scores)
            tops[r, i : i + step_rows] = jnp.broadcast_to(best, acc.shape)
            totals[r, i : i + step_rows] = jnp.broadcast_to(total, acc.shape)
            sums[r, i : i + step_rows] = acc


def attend_kernel(where, q_keep, got, tops, totals, sums, part, mine, send, scores, held, sems):
    scale = HEAD_DIM ** (-0.5)
    step_rows = scores.shape[0]
    hold([part], held, sems)
    for r, out in enumerate((mine, send)):
        for i in range(0, q_keep.shape[2], step_rows):
            best, total, acc = attend_rows(query_rows(q_keep, got, r, i, step_rows), held, scores)
            before = tops[r, i : i + step_rows]
            top = jnp.maximum(before, best)
            old, new = jnp.exp((before - top) * scale), jnp.exp((best - top) * scale)
            total = totals[r, i : i + step_rows] * old + total * new
            out[i : i + step_rows, :] = ((sums[r, i : i + step_rows] * old + acc * new) / total).astype(BF16)


def spread_out(inputs, pairs, places, mine, other, same):
    for (near, far), place in zip(pairs, places):
        a = dot_t(inputs, near).astype(BF16)
        b = dot_t(inputs, far).astype(BF16)
        mine[place] = jnp.where(same, a, b)
        other[place] = jnp.where(same, b, a)


def project_out_kernel(where, own, got, weight, far_weight, mine, other):
    xl = where[1]
    a, b = own[...], got[...]
    heads = jnp.concatenate([jnp.where(xl == 0, a, b), jnp.where(xl == 0, b, a)], axis=1)
    blocks, rows, block = mine.shape
    pairs = [(weight[j * block : (j + 1) * block], far_weight[j * block : (j + 1) * block]) for j in range(blocks)]
    spread_out(heads, pairs, range(blocks), mine, other, where[2] == xl)


def glu_kernel(where, mine, other, gain, *refs):
    pieces, (gated, normed, weights, sems) = refs[:-4], refs[-4:]
    blocks, rows, block = mine.shape
    sources = [piece.at[:4] for piece in pieces]
    sources[4:6] = [pieces[4], pieces[5].at[:1]]
    places = [weights.at[j] for j in range(4)] + [weights.at[4, :3], weights.at[4, 3:]] + [weights.at[j] for j in range(5, 8)]
    copies = fetch(sources, places, sems)
    z, xl = where[0], where[1]
    same = where[2] == xl
    step_rows = 32
    width = 2 * blocks * block

    def chunk(i, carry):
        r = pl.ds(pl.multiple_of(i * step_rows, step_rows), step_rows)
        parts = []
        for j in range(blocks):
            at = lax.rem(z + j, blocks)
            a, b = mine[at, r, :], other[at, r, :]
            parts += [jnp.where(same, a, b).astype(F32), jnp.where(same, b, a).astype(F32)]
        mean = jnp.sum(sum(parts), axis=-1, keepdims=True) / width
        square = sum((p - mean) * (p - mean) for p in parts)
        scale = lax.rsqrt(jnp.sum(square, axis=-1, keepdims=True) / width + 1e-05)
        for n, p in enumerate(parts):
            parity = xl if n % 2 == 0 else 1 - xl
            cols = pl.ds(pl.multiple_of((lax.rem(z + n // 2, blocks) * 2 + parity) * block, block), block)
            normed[n, r, :] = ((p - mean) * scale * gain[:, cols]).astype(BF16)
        return carry

    lax.fori_loop(0, rows // step_rows, chunk, 0)
    for copy in copies:
        copy.wait()
    sums = [None, None]
    for n in range(2 * blocks):
        j = n // 2
        for m in range(2):
            term = dot(normed[n], weights[j, 2 * m + n % 2])
            sums[m] = term if sums[m] is None else sums[m] + term
    gated[...] = (sums[0] * jax.nn.sigmoid(sums[1])).astype(BF16)


def conv_kernel(where, gated, before, after, taps, scale, offset, *refs):
    pieces, (mine, other, padded, activated, weights, sems) = refs[:-6], refs[-6:]
    sources = [piece.at[4:] for n, piece in enumerate(pieces) if n not in (4, 5)]
    sources.append(pieces[5].at[1:])
    copies = fetch(sources, [weights.at[j] for j in (0, 1, 2, 3, 5, 6, 7, 4)], sems)
    rows = gated.shape[0]
    rim = before.shape[0]
    seq = where[0] * 2 + where[1]
    padded[:rim] = jnp.where(seq > 0, before[...].astype(F32), 0.0)
    padded[rim : rim + rows] = gated[...].astype(F32)
    padded[rim + rows :] = jnp.where(seq < where[3] - 1, after[...].astype(F32), 0.0)
    count = taps.shape[0]
    first = rim - (count - 1) // 2
    for i in range(0, rows, 32):
        acc = None
        for k in range(count):
            term = taps[k : k + 1, :] * padded[i + first + k : i + first + k + 32, :]
            acc = term if acc is None else acc + term
        v = acc * scale[...] + offset[...]
        activated[i : i + 32, :] = (v * jax.nn.sigmoid(v)).astype(BF16)
    for copy in copies:
        copy.wait()
    pairs = [(weights[j, 0], weights[j, 1]) for j in range(8)]
    places = [lax.rem(where[0] + j, 8) for j in range(8)]
    spread_out(activated[...], pairs, places, mine, other, where[2] == where[1])


def residual_kernel(where, parts, frames, mixed, copies, held, sem, sems):
    block = mixed.shape[1]
    cols = pl.ds(pl.multiple_of(where[4] * block, block), block)
    copy = pltpu.make_async_copy(frames.at[:, cols], held, sem)
    copy.start()
    total = parts[0].astype(F32)
    for j in range(1, parts.shape[0]):
        total = total + parts[j].astype(F32)
    copy.wait()
    result = (held[...].astype(F32) + total).astype(BF16)
    mixed[...] = result
    count = copies.shape[0]
    for out in fetch([mixed] * count, [copies.at[j] for j in range(count)], sems):
        out.wait()


def both_ways(right, left):
    return shift(right, "z", 1), shift(left, "z", -1)


def pair_sum(mine, other):
    got = shift(other, "c", 1)
    return (mine.astype(F32) + got.astype(F32)).astype(BF16)


def exchange(parts):
    return lax.all_to_all(parts, CHIPS, 0, 0, tiled=True)


def local(
    frames,
    attn_norm_gain,
    qkv_weight,
    attn_out_weight,
    conv_norm_gain,
    glu_weight,
    depth_kernel,
    norm_scale,
    norm_shift,
    conv_out_weight,
):
    rows, width = frames.shape
    block = qkv_weight.shape[2]
    blocks = width // block // 2
    z, xl, core = (lax.axis_index(a) for a in ("z", "xl", "c"))
    where = jnp.stack([z, xl, core, lax.axis_size(SEQ), lax.axis_index(WT)]).astype(jnp.int32)
    S = jax.ShapeDtypeStruct

    step = lax.optimization_barrier
    out_weight = lax.all_gather(attn_out_weight, "z", axis=0, tiled=True)
    late = jnp.concatenate([glu_weight, conv_out_weight[None]])
    late_far = shift(late, "xl", 1)

    half = block // 2
    r1, l1 = both_ways(qkv_weight, qkv_weight)
    mine, other = run_kernel(
        norm_blocks_kernel, where, [frames, attn_norm_gain.reshape(1, width)],
        [S((blocks, rows, block), BF16), S((blocks // 2, rows, block), BF16)], [], 16, 10 * rows * width, 4 * rows * width)
    got = shift(other, "xl", 1)
    r2, l2 = both_ways(r1, l1)
    r3, l3 = both_ways(r2, l2)
    far = both_ways(r3[:, :half], l3[:, half:])
    swapped, late_far = step((shift(got, "c", 1), late_far))
    late = jnp.stack([late, late_far], axis=1).reshape(6, block, block)
    kv_keep, q_keep, send = run_kernel(
        project_kernel, where, [mine, got, swapped],
        [S((2, 2, rows, HEAD_DIM), F32), S((1, 2, rows, HEAD_DIM), F32), S((3, 2, rows, HEAD_DIM), BF16)],
        [pltpu.VMEM((3, blocks, block, block), BF16), pltpu.SemaphoreType.DMA((3, 9))], 60,
        6 * rows * width * block, 6 * block * block * 8 + 4 * rows * width,
        pinned=[qkv_weight, l1, l2, l3, *far, r3, r2, r1])
    got, late = step((shift(send, "xl", 1), late))
    kv = (kv_keep + got[1:, ::-1].astype(F32)).astype(BF16)

    kv_r1, kv_l1 = both_ways(kv, kv)
    kv_r2, kv_l2 = both_ways(kv_r1, kv_l1)
    kv_r3, kv_l3 = both_ways(kv_r2, kv_l2)
    out_weight = [out_weight, shift(out_weight, "xl", 1)]
    kv_r3, kv_l3, late_left = step((kv_r3, kv_l3, late))
    late_l1 = shift(late_left, "z", -1)
    kv_r4 = shift(kv_r3, "z", 1)
    parts = [kv, kv_l1, kv_l2, kv_l3, kv_r3, kv_r2, kv_r1]
    stat = S((2, rows, HEAD_DIM), F32)

    def attend_scratch(count):
        return [pltpu.VMEM((128, 2 * rows * count), F32), pltpu.VMEM((count, 2, 2, rows, HEAD_DIM), BF16), pltpu.SemaphoreType.DMA((count,))]

    tops, totals, sums = run_kernel(
        attend_early_kernel, where, [q_keep, got], [stat] * 3, attend_scratch(len(parts)), 32,
        7 * rows * 16 * rows * HEAD_DIM, 4 << 20, 2 * rows * 14 * rows, pinned=parts)
    kv_r4, late_right, tops, totals, sums = step((kv_r4, late, tops, totals, sums))
    late_r1 = shift(late_right, "z", 1)
    own, away = run_kernel(
        attend_kernel, where, [q_keep, got, tops, totals, sums], [S((rows, HEAD_DIM), BF16)] * 2, attend_scratch(1), 32,
        rows * 16 * rows * HEAD_DIM, 2 << 20, 2 * rows * 2 * rows, pinned=[kv_r4])
    back, late_l1 = step((shift(away, "xl", 1), late_l1))
    blocks_out = [S((blocks, rows, block), BF16)] * 2
    mine, other = run_kernel(
        project_out_kernel, where, [own, back] + out_weight, blocks_out, [], 16,
        2 * rows * block * width, 4 << 20)
    other, late_r1 = step((other, late_r1))
    late_r2, late_l2 = both_ways(late_r1, late_l1)
    late_r3, late_l3 = both_ways(late_r2, late_l2)
    mixed, copies = run_kernel(
        residual_kernel, where, [exchange(pair_sum(mine, other))],
        [S((rows, block), BF16), S((blocks, rows, block), BF16)],
        [pltpu.VMEM((rows, block), BF16), pltpu.SemaphoreType.DMA, pltpu.SemaphoreType.DMA((blocks,))], 16,
        10 * rows * block, 20 * rows * block, pinned=[frames], out_specs=[vmem(), hbm()])
    late_far = both_ways(late_r3[:3], late_l3[3:])
    mine, *late_far = step((exchange(copies), *late_far))
    other = shift(mine, "c", 1)
    late = [late, late_l1, late_l2, late_l3, *late_far, late_r3, late_r2, late_r1]
    gated = run_kernel(
        glu_kernel, where, [mine, other, conv_norm_gain.reshape(1, width)],
        S((rows, block), BF16),
        [pltpu.VMEM((2 * blocks, rows, block), BF16), pltpu.VMEM((blocks, 4, block, block), BF16), pltpu.SemaphoreType.DMA((9,))], 48,
        4 * rows * block * width, 6 << 20, pinned=late)
    rim = 16
    before = shift(gated[rows - rim :], SEQ, 1)
    after = shift(gated[:rim], SEQ, -1)
    mine, other = run_kernel(
        conv_kernel, where,
        [gated, before, after, depth_kernel, norm_scale.reshape(1, block), norm_shift.reshape(1, block)],
        blocks_out,
        [pltpu.VMEM((rows + 2 * rim, block), F32), pltpu.VMEM((rows, block), BF16),
         pltpu.VMEM((blocks, 2, block, block), BF16), pltpu.SemaphoreType.DMA((blocks,))], 16,
        2 * rows * block * width, 4 << 20, pinned=late)
    total = jnp.sum(exchange(pair_sum(mine, other)).astype(F32), axis=0)
    return (mixed.astype(F32) + total).astype(BF16)


def solution(mesh):
    split = Mesh(mesh.devices.reshape(8, 2, 2, 4, 2), ("z", "xl", "xh", "y", "c"))
    in_specs = (
        P(SEQ, None),
        P(),
        P(None, SEQ, WT),
        P(SEQ, WT),
        P(),
        P(None, SEQ, WT),
        P(None, WT),
        P(WT),
        P(WT),
        P(SEQ, WT),
    )
    return jax.shard_map(local, mesh=split, in_specs=in_specs, out_specs=P(SEQ, WT), check_vma=False)
```
